128 devices in a mesh: grp: 16 (over y_lo, z, core), tp: 8 (over x, y_hi).
Axes of the slice: x: 4, y: 4 (y_hi: 2, y_lo: 2; y = y_hi * 2 + y_lo), z: 4, core: 2. Of those that a mesh axis runs over, the one named last changes fastest.
Arguments:
- tokens: bfloat16 [2, 5120, 4096], P(None, 'grp', 'tp'), may hold values from -6 to 6
- norm_gain: float32 [4096], replicated, may hold values from 0.5 to 1.5
- up_master: float32 [4096, 16384], P(('grp', 'tp')), may hold values from -6 to 6
- up_gradient: bfloat16 [4096, 16384], P(('grp', 'tp')), may hold values from -0.59765625 to 0.59765625
- up_first: float32 [4096, 16384], P(('grp', 'tp')), may hold values from -0.18 to 0.18
- up_second: float32 [4096, 16384], P(('grp', 'tp')), may hold values from 0.0001 to 0.01
- down_master: float32 [16384, 4096], P(('grp', 'tp')), may hold values from -6 to 6
- down_gradient: bfloat16 [16384, 4096], P(('grp', 'tp')), may hold values from -0.59765625 to 0.59765625
- down_first: float32 [16384, 4096], P(('grp', 'tp')), may hold values from -0.18 to 0.18
- down_second: float32 [16384, 4096], P(('grp', 'tp')), may hold values from 0.0001 to 0.01
Outputs:
- up_updated: float32 [4096, 16384], P(('grp', 'tp'))
- down_updated: float32 [16384, 4096], P(('grp', 'tp'))
- decoded: bfloat16 [2, 5120, 4096], P(None, 'grp', 'tp')
The draws below stay inside these ranges and needn't reach their ends.
All inputs are finite; a program needn't handle non-finite values.
Results may differ from the reference program's by a relative error of at most 0.015.
Values may be sent and summed in bfloat16 or wider, within the bound.
No kernel may reach another device: no remote copies, remote signals or barrier semaphores. Data moves between devices by JAX's collectives and lax.ppermute only.
A program may use at most 192 MiB of HBM per device.

```python
import math
import jax
import jax.numpy as jnp
from jax import lax

D = 4096
FF = 16384
ROWS = 320
STEPS = 2
GROUP_ROWS = 5120
N_GRP = 16
N_TP = 8


def block_scale(own_key, shape, cuts, smallest, largest):
    level = 1.0
    for position, parts in cuts:
        heights = jax.random.uniform(jax.random.fold_in(jax.random.fold_in(own_key, 6), position), (parts,), jnp.float32, smallest / len(cuts), largest / len(cuts))
        level = level * jnp.repeat(jnp.exp(heights), shape[position] // parts).reshape((-1,) + (1,) * (len(shape) - 1 - position))
    return level


def noise(stream_key, dims, scale, limit, shards=(), dtype=jnp.bfloat16):
    values = scale * jax.random.normal(stream_key, dims, jnp.float32)
    if shards:
        values = values * block_scale(stream_key, dims, shards, -0.22, 0.18)
    return jnp.clip(values, -limit, limit).astype(dtype)


def setup_inputs(seed: int = 0) -> dict:
    seeds = jax.random.split(jax.random.key(seed), 11)
    tokens = noise(seeds[0], (STEPS, GROUP_ROWS, D), 1.0, 6.0, ((1, 16), (2, 8)))
    norm_gain = jnp.clip(1.0 + 0.1 * jax.random.normal(seeds[1], (D,), jnp.float32), 0.5, 1.5)
    up_master = noise(seeds[2], (D, FF), 1.0, 6.0, ((0, 128),), jnp.float32)
    up_gradient = noise(seeds[3], (D, FF), 0.1, 0.59765625, ((0, 128),))
    up_first = noise(seeds[4], (D, FF), 0.03, 0.18, ((0, 128),), jnp.float32)
    up_second = jnp.clip(jnp.exp(math.log(0.01) - 4.6051702 * jax.random.uniform(seeds[5], (D, FF), jnp.float32) ** block_scale(seeds[5], (D, FF), ((0, 128),), -0.2, 0.2)), 0.0001, 0.01)
    down_master = noise(seeds[6], (FF, D), 1.0, 6.0, ((0, 128),), jnp.float32)
    down_gradient = noise(seeds[7], (FF, D), 0.1, 0.59765625, ((0, 128),))
    down_first = noise(seeds[8], (FF, D), 0.03, 0.18, ((0, 128),), jnp.float32)
    down_second = jnp.clip(jnp.exp(math.log(0.01) - 4.6051702 * jax.random.uniform(seeds[9], (FF, D), jnp.float32) ** block_scale(seeds[9], (FF, D), ((0, 128),), -0.2, 0.2)), 0.0001, 0.01)
    return dict(tokens=tokens, norm_gain=norm_gain, up_master=up_master, up_gradient=up_gradient, up_first=up_first, up_second=up_second, down_master=down_master, down_gradient=down_gradient, down_first=down_first, down_second=down_second)


learn_rate = 0.05
beta_one = 0.9
beta_two = 0.95
adam_eps = 1e-08
decay_rate = 0.1
step_index = 100
norm_eps = 1e-06

def adamw_update(master, gradient, first_moment, second_moment):
    grad_float = gradient.astype(jnp.float32)
    first_new = beta_one * first_moment + (1.0 - beta_one) * grad_float
    second_new = beta_two * second_moment + (1.0 - beta_two) * grad_float * grad_float
    corr_one = 1.0 - beta_one ** step_index
    corr_two = 1.0 - beta_two ** step_index
    update = first_new / corr_one / (jnp.sqrt(second_new / corr_two) + adam_eps)
    return master - learn_rate * (update + decay_rate * master)

def reference(tokens, norm_gain, up_master, up_gradient, up_first, up_second, down_master, down_gradient, down_first, down_second):
    up_updated = adamw_update(up_master, up_gradient, up_first, up_second)
    down_updated = adamw_update(down_master, down_gradient, down_first, down_second)
    up_cast = up_updated.astype(jnp.bfloat16)
    down_cast = down_updated.astype(jnp.bfloat16)
    block_width = FF // (N_GRP * N_TP)
    up_split = up_cast.reshape(D, N_GRP, N_TP, block_width)
    down_split = down_cast.reshape(N_GRP, N_TP, block_width, D)

    def one_group(group_rows):
        flat_rows = group_rows.reshape(STEPS * ROWS, D).astype(jnp.float32)
        mean_sq = lax.optimization_barrier(jnp.mean(flat_rows * flat_rows, axis=-1, keepdims=True))
        normed = (flat_rows * lax.rsqrt(mean_sq + norm_eps) * norm_gain).astype(jnp.bfloat16)
        running = jnp.zeros((STEPS * ROWS, D), jnp.float32)
        for class_index in range(N_TP):
            up_class = up_split[:, :, class_index, :].reshape(D, N_GRP * block_width)
            hidden = jax.nn.silu(jnp.dot(normed, up_class, preferred_element_type=jnp.float32) * D ** (-0.5)).astype(jnp.bfloat16)
            down_class = down_split[:, class_index].reshape(N_GRP * block_width, D)
            partial_value = (jnp.dot(hidden, down_class, preferred_element_type=jnp.float32) * FF ** (-0.5)).astype(jnp.bfloat16)
            running = running + partial_value.astype(jnp.float32)
        return running.astype(jnp.bfloat16).reshape(STEPS, ROWS, D)
    grouped = tokens.reshape(STEPS, N_GRP, ROWS, D).transpose(1, 0, 2, 3)
    results = lax.map(one_group, grouped)
    decoded = results.transpose(1, 0, 2, 3).reshape(STEPS, N_GRP * ROWS, D)
    return (up_updated, down_updated, decoded)
```

```python
import functools

import jax
import jax.numpy as jnp
import numpy as np
from jax import lax
from jax.experimental import pallas as pl
from jax.experimental.pallas import tpu as pltpu
from jax.sharding import Mesh, PartitionSpec as P

learn_rate = 0.05
beta_one = 0.9
beta_two = 0.95
adam_eps = 1e-08
decay_rate = 0.1
step_index = 100
norm_eps = 1e-06

AXES = ("ylo", "z", "core", "x", "yhi")
SIZES = (2, 4, 2, 4, 2)
D, FF = 4096, 16384
CHUNKS = 4
ORDER = ((0, 0), (1, 0), (0, 3), (0, 1), (0, 2), (1, 3), (1, 1), (1, 2))
PLACE = {o: k for k, o in enumerate(ORDER)}
MIB = 1 << 20


def shifted(**steps):
    pairs = []
    for i, c in enumerate(np.ndindex(*SIZES)):
        d = dict(zip(AXES, c))
        for a, s in steps.items():
            d[a] = (d[a] + s) % SIZES[AXES.index(a)]
        pairs.append((i, int(np.ravel_multi_index(tuple(d[a] for a in AXES), SIZES))))
    return pairs


def send(v, **steps):
    return lax.ppermute(v, AXES, shifted(**steps))


def adamw(master, gradient, first_moment, second_moment):
    grad_float = gradient.astype(jnp.float32)
    first_new = beta_one * first_moment + (1.0 - beta_one) * grad_float
    second_new = beta_two * second_moment + (1.0 - beta_two) * grad_float * grad_float
    corr_one = 1.0 - beta_one**step_index
    corr_two = 1.0 - beta_two**step_index
    update = first_new * (1.0 / corr_one) / (jnp.sqrt(second_new * (1.0 / corr_two)) + adam_eps)
    return master - learn_rate * (update + decay_rate * master)


def params(limit=24, sem=None):
    return pltpu.CompilerParams(vmem_limit_bytes=limit * MIB)


def cost(flops, nbytes):
    return pl.CostEstimate(flops=int(flops), bytes_accessed=int(nbytes), transcendentals=0)


def up_kernel(s_ref, w_ref, g_ref, m_ref, v_ref, o_ref, mine_ref, other_ref):
    new = adamw(w_ref[...], g_ref[...], m_ref[...], v_ref[...])
    o_ref[...] = new
    cast = new.astype(jnp.bfloat16)

    def put(lo_ref, hi_ref):
        for t in range(8):
            lo_ref[t] = cast[:, t * 128 : (t + 1) * 128]
            hi_ref[t] = cast[:, 1024 + t * 128 : 1024 + (t + 1) * 128]

    @pl.when(s_ref[0] == 0)
    def _():
        put(mine_ref, other_ref)

    @pl.when(s_ref[0] == 1)
    def _():
        put(other_ref, mine_ref)


def up_step(core, w, g, m, v):
    spec = pl.BlockSpec((32, 2048), lambda i, s: (0, i))
    piece = pl.BlockSpec((8, 32, 128), lambda i, s: (0, 0, i))
    half = jax.ShapeDtypeStruct((8, 32, 1024), jnp.bfloat16)
    return pl.pallas_call(
        up_kernel,
        out_shape=(jax.ShapeDtypeStruct((32, FF), jnp.float32), half, half),
        grid_spec=pltpu.PrefetchScalarGridSpec(
            num_scalar_prefetch=1, grid=(8,), in_specs=[spec] * 4, out_specs=(spec, piece, piece)
        ),
        compiler_params=params(),
        cost_estimate=cost(30 * 32 * FF, 20 * 32 * FF),
        name="adam_up",
    )(core, w, g, m, v)


def down_kernel(w_ref, g_ref, m_ref, v_ref, o_ref, *d_refs):
    new = adamw(w_ref[...], g_ref[...], m_ref[...], v_ref[...])
    o_ref[...] = new
    cast = new.astype(jnp.bfloat16)
    for t in range(8):
        for j in range(CHUNKS):
            d_refs[j][:, t * 128 : (t + 1) * 128] = cast[:, t * 512 + j * 128 : t * 512 + (j + 1) * 128]


def down_step(w, g, m, v):
    spec = pl.BlockSpec((32, D), lambda i: (i, 0))
    chunk = pl.BlockSpec((32, 1024), lambda i: (i, 0))
    return pl.pallas_call(
        down_kernel,
        out_shape=(jax.ShapeDtypeStruct((128, D), jnp.float32),)
        + (jax.ShapeDtypeStruct((128, 1024), jnp.bfloat16),) * CHUNKS,
        grid=(4,),
        in_specs=[spec] * 4,
        out_specs=(spec,) + (chunk,) * CHUNKS,
        compiler_params=params(),
        cost_estimate=cost(30 * 128 * D, 20 * 128 * D),
        name="adam_down",
    )(w, g, m, v)


RELS = tuple((dx, dy) for dx in range(4) for dy in range(2))


def route_kernel(s_ref, mine_ref, recv_ref, *out_refs):
    core, x, yhi = s_ref[0], s_ref[1], s_ref[2]
    for (dx, dy), out in zip(RELS, out_refs):
        t = lax.rem(x + dx, 4) * 2 + lax.rem(yhi + dy, 2)
        out[core] = mine_ref[t]
        out[1 - core] = recv_ref[t]


def route(scalars, mine, recv):
    vm = pl.BlockSpec(memory_space=pltpu.VMEM)
    return pl.pallas_call(
        route_kernel,
        out_shape=(jax.ShapeDtypeStruct((2, 32, 1024), jnp.bfloat16),) * 8,
        in_specs=[pl.BlockSpec(memory_space=pltpu.SMEM), vm, vm],
        out_specs=(vm,) * 8,
        compiler_params=params(),
        cost_estimate=cost(0, 4 * MIB),
        name="route_up",
    )(scalars, mine, recv)


def place_kernel(s_ref, *refs):
    x, yhi = s_ref[1], s_ref[2]
    out = refs[-1]
    for (dx, dy), piece in zip(RELS, refs):
        t = lax.rem(x - dx + 4, 4) * 2 + lax.rem(yhi + dy, 2)
        out[0, t] = piece[0]
        out[1, t] = piece[1]


def place(scalars, pieces):
    vm = pl.BlockSpec(memory_space=pltpu.VMEM)
    out = pl.pallas_call(
        place_kernel,
        out_shape=jax.ShapeDtypeStruct((2, 8, 32, 1024), jnp.bfloat16),
        in_specs=[pl.BlockSpec(memory_space=pltpu.SMEM)] + [vm] * 8,
        out_specs=vm,
        compiler_params=params(),
        cost_estimate=cost(0, 4 * MIB),
        name="place_up",
    )(scalars, *pieces)
    return out.reshape(512, 1024)


def gather(p0):
    half = p0.shape[0] // 2
    p1 = send(p0, ylo=1)
    from_low, from_high = send(p0, z=1), send(p0, z=-1)
    opp = (send(from_low[:half], z=1), send(from_high[half:], z=-1))
    low1, high1 = send(p1, z=1), send(p1, z=-1)
    opp1 = (send(low1[:half], z=1), send(high1[half:], z=-1))
    return [p0, p1, from_low, from_high, *opp, low1, high1, *opp1]


PARTS = ((0, 0), (1, 0), (2, 0), (3, 0), (4, 0), (4, 1), (5, 0), (6, 0), (7, 0), (7, 1))


def hidden_kernel(s_ref, *refs):
    lhs, ws = refs[:8], refs[8:18]
    out, acc = refs[18], refs[19]
    for n, ((k, part), w) in enumerate(zip(PARTS, ws)):
        rows = w.shape[0]
        term = jnp.dot(lhs[k][0, :, part * rows : (part + 1) * rows], w[...], preferred_element_type=jnp.float32)
        if n == 0:
            acc[...] = term
        else:
            acc[...] += term
    for q in range(8):
        u = acc[:, q * 128 : (q + 1) * 128] * D ** (-0.5)
        at = pl.multiple_of(s_ref[8 + q] * 128, 128)
        out[:, pl.ds(at, 128)] = (u / (1.0 + jnp.exp(-u))).astype(jnp.bfloat16)


def hidden_of(scalars, normed, ws):
    rows = 320
    specs = [
        pl.BlockSpec((1, rows, 512), functools.partial(lambda k, i, s: (s[k], i, 0), k)) for k in range(8)
    ]
    specs += [pl.BlockSpec(w.shape, lambda i, s: (0, 0), pipeline_mode=pl.Buffered(1)) for w in ws]
    return pl.pallas_call(
        hidden_kernel,
        out_shape=jax.ShapeDtypeStruct((640, 1024), jnp.bfloat16),
        grid_spec=pltpu.PrefetchScalarGridSpec(
            num_scalar_prefetch=1,
            grid=(640 // rows,),
            in_specs=specs,
            out_specs=pl.BlockSpec((rows, 1024), lambda i, s: (i, 0)),
            scratch_shapes=[pltpu.VMEM((rows, 1024), jnp.float32)],
        ),
        compiler_params=params(32),
        cost_estimate=cost(2 * 640 * 1024 * 4096, 14 * MIB),
        name="hidden",
    )(scalars, *([normed] * 8), *ws)


def partial_kernel(own_ref, sib_ref, *refs):
    ws, (own_out, sib_out, w_ref) = refs[:10], refs[10:]

    @pl.when(pl.program_id(0) == 0)
    def _():
        for (k, part), w in zip(PARTS, ws):
            rows = w.shape[0]
            w_ref[k * 128 + part * rows : k * 128 + (part + 1) * rows] = w[...]

    for src, dst in ((sib_ref, sib_out), (own_ref, own_out)):
        term = jnp.dot(src[...], w_ref[...], preferred_element_type=jnp.float32)
        term = (term * FF ** (-0.5)).astype(jnp.bfloat16)
        for xi in range(4):
            dst[xi] = term[:, xi * 256 : (xi + 1) * 256]


def partial_of(own, sib, ws):
    rows = 320
    block = pl.BlockSpec((rows, 1024), lambda i: (i, 0))
    out = pl.BlockSpec((4, rows, 256), lambda i: (0, i, 0))
    shape = jax.ShapeDtypeStruct((4, 640, 256), jnp.bfloat16)
    return pl.pallas_call(
        partial_kernel,
        out_shape=(shape, shape),
        grid=(640 // rows,),
        in_specs=[block, block]
        + [pl.BlockSpec(w.shape, lambda i: (0, 0), pipeline_mode=pl.Buffered(1)) for w in ws],
        out_specs=(out, out),
        scratch_shapes=[pltpu.VMEM((1024, 1024), jnp.bfloat16)],
        compiler_params=params(24),
        cost_estimate=cost(4 * 640 * 1024 * 1024, 8 * MIB),
        name="partial",
    )(own, sib, *ws)


def body(
    tokens,
    norm_gain,
    up_master,
    up_gradient,
    up_first,
    up_second,
    down_master,
    down_gradient,
    down_first,
    down_second,
):
    ylo, z, core, x, yhi = (lax.axis_index(a) for a in AXES)
    scalars = jnp.stack([core, x, yhi]).astype(jnp.int32)

    tokens_b = send(tokens, yhi=1)
    feats_a = lax.all_gather(tokens, "x", axis=0)
    feats_b = lax.all_gather(tokens_b, "x", axis=0)

    up_updated, mine, other = up_step(scalars[:1], up_master, up_gradient, up_first, up_second)
    recv = send(other, core=1)
    down_updated, *down_chunks = down_step(down_master, down_gradient, down_first, down_second)

    routed = route(scalars, mine, recv)
    moved = [routed[0]] + [send(r, x=dx, yhi=dy) for (dx, dy), r in zip(RELS[1:], routed[1:])]
    ws_up = gather(place(scalars, moved))
    ws_down = [gather(d) for d in down_chunks]

    fa = feats_a.reshape(4, 640, 512).astype(jnp.float32)
    fb = feats_b.reshape(4, 640, 512).astype(jnp.float32)
    total = jnp.sum(fa * fa, axis=(0, 2)) + jnp.sum(fb * fb, axis=(0, 2))
    scale = lax.rsqrt(total * (1.0 / D) + norm_eps)[None, :, None]
    gains = norm_gain.reshape(4, 2, 1, 512)
    ga = lax.dynamic_index_in_dim(gains, yhi, 1, keepdims=False)
    gb = lax.dynamic_index_in_dim(gains, 1 - yhi, 1, keepdims=False)
    normed = jnp.concatenate(
        [(fa * scale * ga).astype(jnp.bfloat16), (fb * scale * gb).astype(jnp.bfloat16)], axis=0
    )
    normed_sib = send(normed, core=1)

    q = jnp.stack([(ylo ^ dy) * 4 + lax.rem(z + dz, 4) for dy, dz in ORDER])
    slots = ((q % 2) ^ yhi) * 4 + q // 2
    table = jnp.array([[PLACE[(a, b)] for b in range(4)] for a in range(2)], jnp.int32)
    goes = jnp.stack([table[a ^ ylo, lax.rem(b - z + 4, 4)] for a in range(2) for b in range(4)])
    where = jnp.concatenate([slots, goes]).astype(jnp.int32)
    hidden_own = hidden_of(where, normed, ws_up)
    hidden_sib = hidden_of(where, normed_sib, ws_up)

    pieces = []
    for ws in ws_down:
        part, part_sib = partial_of(hidden_own, hidden_sib, ws)
        both = part.astype(jnp.float32) + send(part_sib, core=1).astype(jnp.float32)
        rows = lax.psum_scatter(both.astype(jnp.bfloat16), "x", scatter_dimension=0, tiled=True)[0]
        keep = lax.dynamic_slice_in_dim(rows, yhi * 128, 128, 1)
        give = lax.dynamic_slice_in_dim(rows, (1 - yhi) * 128, 128, 1)
        got = send(give, yhi=1)
        pieces.append((keep.astype(jnp.float32) + got.astype(jnp.float32)).astype(jnp.bfloat16))
    decoded = jnp.concatenate(pieces, axis=1).reshape(2, 320, 512)
    return (up_updated, down_updated, decoded)


def solution(mesh):
    fine = Mesh(mesh.devices.reshape(SIZES), AXES)
    grp, tp = AXES[:3], AXES[3:]
    flat = P(AXES, None)
    in_specs = (P(None, grp, tp), P()) + (flat,) * 8
    out_specs = (flat, flat, P(None, grp, tp))
    return jax.shard_map(body, mesh=fine, in_specs=in_specs, out_specs=out_specs, check_vma=False)
```

```python
import functools

import jax
import jax.numpy as jnp
import numpy as np
from jax import lax
from jax.experimental import pallas as pl
from jax.experimental.pallas import tpu as pltpu
from jax.sharding import Mesh, PartitionSpec as P

learn_rate = 0.05
beta_one = 0.9
beta_two = 0.95
adam_eps = 1e-08
decay_rate = 0.1
step_index = 100
norm_eps = 1e-06

AXES = ("ylo", "z", "core", "x", "yhi")
SIZES = (2, 4, 2, 4, 2)
D, FF = 4096, 16384
CHUNKS = 4
ORDER = ((0, 0), (1, 0), (0, 3), (1, 3), (0, 1), (1, 1), (0, 2), (1, 2))
PLACE = {o: k for k, o in enumerate(ORDER)}
MIB = 1 << 20


def shifted(**steps):
    pairs = []
    for i, c in enumerate(np.ndindex(*SIZES)):
        d = dict(zip(AXES, c))
        for a, s in steps.items():
            d[a] = (d[a] + s) % SIZES[AXES.index(a)]
        pairs.append((i, int(np.ravel_multi_index(tuple(d[a] for a in AXES), SIZES))))
    return pairs


def send(v, **steps):
    return lax.ppermute(v, AXES, shifted(**steps))


ANY = pl.BlockSpec(memory_space=pl.ANY)


def after(v, *deps):
    return pl.pallas_call(
        lambda *refs: None,
        out_shape=jax.ShapeDtypeStruct(v.shape, v.dtype),
        in_specs=[ANY] * (1 + len(deps)),
        out_specs=ANY,
        input_output_aliases={0: 0},
        cost_estimate=pl.CostEstimate(flops=0, bytes_accessed=0, transcendentals=0),
        name="after",
    )(v, *deps)


def adamw(master, gradient, first_moment, second_moment):
    grad_float = gradient.astype(jnp.float32)
    first_new = beta_one * first_moment + (1.0 - beta_one) * grad_float
    second_new = beta_two * second_moment + (1.0 - beta_two) * grad_float * grad_float
    corr_one = 1.0 - beta_one**step_index
    corr_two = 1.0 - beta_two**step_index
    update = first_new * (1.0 / corr_one) / (jnp.sqrt(second_new * (1.0 / corr_two)) + adam_eps)
    return master - learn_rate * (update + decay_rate * master)


def params(limit=24, sem=None):
    return pltpu.CompilerParams(vmem_limit_bytes=limit * MIB)


def cost(flops, nbytes):
    return pl.CostEstimate(flops=int(flops) // 1000, bytes_accessed=int(nbytes) // 1000, transcendentals=0)


def up_kernel(s_ref, w_ref, g_ref, m_ref, v_ref, o_ref, mine_ref, other_ref):
    new = adamw(w_ref[...], g_ref[...], m_ref[...], v_ref[...])
    o_ref[...] = new
    cast = new.astype(jnp.bfloat16)

    def put(lo_ref, hi_ref):
        for t in range(8):
            lo_ref[t] = cast[:, t * 128 : (t + 1) * 128]
            hi_ref[t] = cast[:, 1024 + t * 128 : 1024 + (t + 1) * 128]

    @pl.when(s_ref[0] == 0)
    def _():
        put(mine_ref, other_ref)

    @pl.when(s_ref[0] == 1)
    def _():
        put(other_ref, mine_ref)


def up_step(core, w, g, m, v):
    spec = pl.BlockSpec((32, 2048), lambda i, s: (0, i))
    piece = pl.BlockSpec((8, 32, 128), lambda i, s: (0, 0, i))
    half = jax.ShapeDtypeStruct((8, 32, 1024), jnp.bfloat16)
    return pl.pallas_call(
        up_kernel,
        out_shape=(jax.ShapeDtypeStruct((32, FF), jnp.float32), half, half),
        grid_spec=pltpu.PrefetchScalarGridSpec(
            num_scalar_prefetch=1, grid=(8,), in_specs=[spec] * 4, out_specs=(spec, piece, piece)
        ),
        compiler_params=params(),
        cost_estimate=cost(30 * 32 * FF, 20 * 32 * FF),
        name="adam_up",
    )(core, w, g, m, v)


def down_kernel(w_ref, g_ref, m_ref, v_ref, o_ref, first_ref, rest_ref):
    new = adamw(w_ref[...], g_ref[...], m_ref[...], v_ref[...])
    o_ref[...] = new
    cast = new.astype(jnp.bfloat16)
    for t in range(8):
        for j in range(CHUNKS):
            piece = cast[:, t * 512 + j * 128 : t * 512 + (j + 1) * 128]
            if j == 0:
                first_ref[:, t * 128 : (t + 1) * 128] = piece
            else:
                rest_ref[j - 1, :, t * 128 : (t + 1) * 128] = piece


def down_step(w, g, m, v):
    spec = pl.BlockSpec((32, D), lambda i: (i, 0))
    chunk = pl.BlockSpec((32, 1024), lambda i: (i, 0))
    return pl.pallas_call(
        down_kernel,
        out_shape=(
            jax.ShapeDtypeStruct((128, D), jnp.float32),
            jax.ShapeDtypeStruct((128, 1024), jnp.bfloat16),
            jax.ShapeDtypeStruct((CHUNKS - 1, 128, 1024), jnp.bfloat16),
        ),
        grid=(4,),
        in_specs=[spec] * 4,
        out_specs=(spec, chunk, pl.BlockSpec((CHUNKS - 1, 32, 1024), lambda i: (0, i, 0))),
        compiler_params=params(),
        cost_estimate=cost(30 * 128 * D, 20 * 128 * D),
        name="adam_down",
    )(w, g, m, v)


RELS = tuple((dx, dy) for dx in range(4) for dy in range(2))


def route_kernel(s_ref, mine_ref, recv_ref, dep_ref, *out_refs):
    core, x, yhi = s_ref[0], s_ref[1], s_ref[2]
    for (dx, dy), out in zip(RELS, out_refs):
        t = lax.rem(x + dx, 4) * 2 + lax.rem(yhi + dy, 2)
        out[core] = mine_ref[t]
        out[1 - core] = recv_ref[t]


def route(scalars, mine, recv, dep):
    vm = pl.BlockSpec(memory_space=pltpu.VMEM)
    return pl.pallas_call(
        route_kernel,
        out_shape=(jax.ShapeDtypeStruct((2, 32, 1024), jnp.bfloat16),) * 8,
        in_specs=[pl.BlockSpec(memory_space=pltpu.SMEM), vm, vm, ANY],
        out_specs=(vm,) * 8,
        compiler_params=params(),
        cost_estimate=cost(0, 4 * MIB),
        name="route_up",
    )(scalars, mine, recv, dep)


def place_kernel(s_ref, *refs):
    x, yhi = s_ref[1], s_ref[2]
    out = refs[-1]
    for (dx, dy), piece in zip(RELS, refs):
        t = lax.rem(x - dx + 4, 4) * 2 + lax.rem(yhi + dy, 2)
        out[0, t] = piece[0]
        out[1, t] = piece[1]


def place(scalars, pieces, deps):
    vm = pl.BlockSpec(memory_space=pltpu.VMEM)
    out = pl.pallas_call(
        place_kernel,
        out_shape=jax.ShapeDtypeStruct((2, 8, 32, 1024), jnp.bfloat16),
        in_specs=[pl.BlockSpec(memory_space=pltpu.SMEM)] + [vm] * 8 + [ANY] * len(deps),
        out_specs=vm,
        compiler_params=params(),
        cost_estimate=cost(0, 4 * MIB),
        name="place_up",
    )(scalars, *pieces, *deps)
    return out.reshape(512, 1024)


def both_ways(up, down):
    return send(up, z=1), send(down, z=-1)


def norm_kernel(a_ref, b_ref, g_ref, *refs):
    out = refs[-1]
    total = 0.0
    for ref in (a_ref, b_ref):
        for i in range(4):
            f = ref[i].astype(jnp.float32)
            total += jnp.sum(f * f, axis=-1, keepdims=True)
    scale = lax.rsqrt(total * (1.0 / D) + norm_eps)
    for n, ref in enumerate((a_ref, b_ref)):
        for i in range(4):
            gain = g_ref[n * 4 + i : n * 4 + i + 1]
            out[n * 4 + i] = (ref[i].astype(jnp.float32) * scale * gain).astype(jnp.bfloat16)


def norm_of(feats_a, feats_b, gains, deps):
    rows = 160
    block = pl.BlockSpec((4, rows, 512), lambda i: (0, i, 0))
    return pl.pallas_call(
        norm_kernel,
        out_shape=jax.ShapeDtypeStruct((8, 640, 512), jnp.bfloat16),
        grid=(640 // rows,),
        in_specs=[block, block, pl.BlockSpec((8, 512), lambda i: (0, 0))] + [ANY] * len(deps),
        out_specs=pl.BlockSpec((8, rows, 512), lambda i: (0, i, 0)),
        compiler_params=params(32),
        cost_estimate=cost(8 * 640 * D, 10 * MIB),
        name="norm",
    )(feats_a, feats_b, gains, *deps)


def silu(u):
    return u / (1.0 + jnp.exp(-u))


def first_kernel(s_ref, *refs):
    lhs, ws, acc = refs[:6], refs[6:12], refs[12]
    for k, (a, w) in enumerate(zip(lhs, ws)):
        term = jnp.dot(a[0], w[...], preferred_element_type=jnp.float32)
        if k == 0:
            acc[...] = term
        else:
            acc[...] += term


def last_kernel(s_ref, acc_ref, *refs):
    lhs, ws, out, acc = refs[:2], refs[2:6], refs[6], refs[7]
    acc[...] = acc_ref[...]
    for n, w in enumerate(ws):
        a = lhs[n // 2][0, :, (n % 2) * 256 : (n % 2 + 1) * 256]
        acc[...] += jnp.dot(a, w[...], preferred_element_type=jnp.float32)
    for q in range(8):
        u = acc[:, q * 128 : (q + 1) * 128] * D ** (-0.5)
        at = pl.multiple_of(s_ref[8 + q] * 128, 128)
        out[:, pl.ds(at, 128)] = silu(u).astype(jnp.bfloat16)


def hidden_specs(places, ws):
    rows = 320
    lhs = [pl.BlockSpec((1, rows, 512), functools.partial(lambda k, i, s: (s[k], i, 0), k)) for k in places]
    return lhs, [pl.BlockSpec(w.shape, lambda i, s: (0, 0), pipeline_mode=pl.Buffered(1)) for w in ws]


def hidden_first(scalars, normed, ws):
    lhs, rhs = hidden_specs(range(6), ws)
    return pl.pallas_call(
        first_kernel,
        out_shape=jax.ShapeDtypeStruct((640, 1024), jnp.float32),
        grid_spec=pltpu.PrefetchScalarGridSpec(
            num_scalar_prefetch=1,
            grid=(2,),
            in_specs=lhs + rhs,
            out_specs=pl.BlockSpec((320, 1024), lambda i, s: (i, 0)),
        ),
        compiler_params=params(32),
        cost_estimate=cost(2 * 640 * 1024 * 3072, 14 * MIB),
        name="hidden_first",
    )(scalars, *([normed] * 6), *ws)


def hidden_last(scalars, acc, normed, ws):
    lhs, rhs = hidden_specs((6, 7), ws)
    block = pl.BlockSpec((320, 1024), lambda i, s: (i, 0))
    return pl.pallas_call(
        last_kernel,
        out_shape=jax.ShapeDtypeStruct((640, 1024), jnp.bfloat16),
        grid_spec=pltpu.PrefetchScalarGridSpec(
            num_scalar_prefetch=1,
            grid=(2,),
            in_specs=[block] + lhs + rhs,
            out_specs=block,
            scratch_shapes=[pltpu.VMEM((320, 1024), jnp.float32)],
        ),
        compiler_params=params(32),
        cost_estimate=cost(2 * 640 * 1024 * 1024, 8 * MIB),
        name="hidden_last",
    )(scalars, acc, normed, normed, *ws)


def partial_kernel(s_ref, own_ref, sib_ref, *refs):
    ws, (own_out, sib_out, w_ref) = refs[:5], refs[-3:]

    @pl.when(pl.program_id(0) == 0)
    def _():
        at = 0
        for w in ws:
            w_ref[at : at + w.shape[0]] = w[...]
            at += w.shape[0]

    for src, dst in ((sib_ref, sib_out), (own_ref, own_out)):
        term = jnp.dot(src[...], w_ref[...], preferred_element_type=jnp.float32)
        term = (term * FF ** (-0.5)).astype(jnp.bfloat16)
        for xi in range(4):
            dst[s_ref[xi]] = term[:, xi * 256 : (xi + 1) * 256]


def partial_of(scalars, own, sib, ws, deps):
    rows = 320
    block = pl.BlockSpec((rows, 1024), lambda i, s: (i, 0))
    out = pl.BlockSpec((4, rows, 256), lambda i, s: (0, i, 0))
    shape = jax.ShapeDtypeStruct((4, 640, 256), jnp.bfloat16)
    return pl.pallas_call(
        partial_kernel,
        out_shape=(shape, shape),
        grid_spec=pltpu.PrefetchScalarGridSpec(
            num_scalar_prefetch=1,
            grid=(640 // rows,),
            in_specs=[block, block]
            + [pl.BlockSpec(w.shape, lambda i, s: (0, 0), pipeline_mode=pl.Buffered(1)) for w in ws]
            + [ANY] * len(deps),
            out_specs=(out, out),
            scratch_shapes=[pltpu.VMEM((1024, 1024), jnp.bfloat16)],
        ),
        compiler_params=params(24),
        cost_estimate=cost(4 * 640 * 1024 * 1024, 8 * MIB),
        name="partial",
    )(scalars, own, sib, *ws, *deps)


def body(
    tokens,
    norm_gain,
    up_master,
    up_gradient,
    up_first,
    up_second,
    down_master,
    down_gradient,
    down_first,
    down_second,
):
    ylo, z, core, x, yhi = (lax.axis_index(a) for a in AXES)
    scalars = jnp.stack([core, x, yhi]).astype(jnp.int32)

    tokens_b = send(tokens, yhi=1)
    feats_a = lax.all_gather(tokens, "x", axis=0)

    up_updated, mine, other = up_step(scalars[:1], up_master, up_gradient, up_first, up_second)
    recv = send(other, core=1)
    down_updated, down_a, down_b = down_step(down_master, down_gradient, down_first, down_second)
    ylo_a, ylo_b = send(down_a, ylo=1), send(down_b, ylo=1)

    routed = route(scalars, mine, recv, down_updated)
    moved = [routed[0]] + [send(r, x=dx, yhi=dy) for (dx, dy), r in zip(RELS[1:], routed[1:])]
    st = jnp.concatenate([down_a, ylo_a], axis=0)
    low, high = both_ways(st, st)
    ws_down = [[st, low, high, *both_ways(low[:128], high[128:])]]

    u0 = place(scalars, moved, (low, high))
    feats_b = lax.all_gather(after(tokens_b, u0), "x", axis=0)

    u1 = send(u0, ylo=1)
    low0, high0 = both_ways(u0, u0)
    opp0 = both_ways(after(low0[:256], u1, ylo_b, *ws_down[0][3:]), high0[256:])
    low1, high1 = both_ways(u1, u1)
    opp1 = both_ways(low1[:256], high1[256:])

    gains = norm_gain.reshape(4, 2, 512)
    gains = jnp.concatenate(
        [lax.dynamic_index_in_dim(gains, k, 1, keepdims=False) for k in (yhi, 1 - yhi)], axis=0
    )
    normed = norm_of(feats_a.reshape(4, 640, 512), feats_b.reshape(4, 640, 512), gains, (low1, high1, *opp0))
    normed_sib = send(normed, core=1)

    q = jnp.stack([(ylo ^ dy) * 4 + lax.rem(z + dz, 4) for dy, dz in ORDER])
    slots = ((q % 2) ^ yhi) * 4 + q // 2
    table = jnp.array([[PLACE[(a, b)] for b in range(4)] for a in range(2)], jnp.int32)
    goes = jnp.stack([table[a ^ ylo, lax.rem(b - z + 4, 4)] for a in range(2) for b in range(4)])
    where = jnp.concatenate([slots, goes]).astype(jnp.int32)
    ws_up = (u0, u1, low0, low1, high0, high1)
    firsts = [hidden_first(where, n, ws_up) for n in (normed, normed_sib)]
    hidden_own, hidden_sib = (
        hidden_last(where, f, n, opp0 + opp1) for f, n in zip(firsts, (normed, normed_sib))
    )

    pieces, sums, reduced = [], [], []
    places = jnp.arange(4, dtype=jnp.int32)

    def fetch(j, first, second):
        st = after(jnp.concatenate([down_b[j - 1], ylo_b[j - 1]], axis=0), *first)
        low, high = both_ways(st, st)
        up, down = low[:128], high[128:]
        if second:
            up = after(up, *second)
        ws_down.append([st, low, high, *both_ways(up, down)])

    def multiply(j):
        direct = j % 2 == 1
        deps = sums[-1:]
        if j + 1 < CHUNKS:
            deps += ws_down[j + 1][1:3]
        if j >= 2:
            deps += reduced[j - 2 : j - 1]
        part, part_sib = partial_of(
            (places - x) % 4 if direct else places, hidden_own, hidden_sib, ws_down[j], deps
        )
        part_sib = send(part_sib, core=1)
        add = lambda a, b: (a.astype(jnp.float32) + b.astype(jnp.float32)).astype(jnp.bfloat16)
        if direct:
            terms = [add(part[d], part_sib[d]) for d in range(4)]
            sums.append(terms[1])
            terms = terms[:1] + [send(terms[d], x=d) for d in (1, 2, 3)]
            rows = sum(v.astype(jnp.float32) for v in terms).astype(jnp.bfloat16)
        else:
            both = add(part, part_sib)
            sums.append(both)
            rows = lax.psum_scatter(both, "x", scatter_dimension=0, tiled=True)[0]
        reduced.append(rows)
        keep = lax.dynamic_slice_in_dim(rows, yhi * 128, 128, 1)
        give = lax.dynamic_slice_in_dim(rows, (1 - yhi) * 128, 128, 1)
        pieces.append(add(keep, send(give, yhi=1)))

    fetch(1, (low1,), ())
    fetch(2, opp1, ())
    multiply(0)
    fetch(3, ws_down[1][3:], sums[:1])
    multiply(1)
    multiply(2)
    multiply(3)
    decoded = jnp.concatenate(pieces, axis=1).reshape(2, 320, 512)
    return (up_updated, down_updated, decoded)


def solution(mesh):
    fine = Mesh(mesh.devices.reshape(SIZES), AXES)
    grp, tp = AXES[:3], AXES[3:]
    flat = P(AXES, None)
    in_specs = (P(None, grp, tp), P()) + (flat,) * 8
    out_specs = (flat, flat, P(None, grp, tp))
    return jax.shard_map(body, mesh=fine, in_specs=in_specs, out_specs=out_specs, check_vma=False)
```

```python
import functools

import jax
import jax.numpy as jnp
import numpy as np
from jax import lax
from jax.experimental import pallas as pl
from jax.experimental.pallas import tpu as pltpu
from jax.sharding import Mesh, PartitionSpec as P

learn_rate = 0.05
beta_one = 0.9
beta_two = 0.95
adam_eps = 1e-08
decay_rate = 0.1
step_index = 100
norm_eps = 1e-06

AXES = ("ylo", "z", "core", "x", "yhi")
SIZES = (2, 4, 2, 4, 2)
D, FF = 4096, 16384
CHUNKS = 4
ORDER = ((0, 0), (1, 0), (0, 3), (1, 3), (0, 1), (1, 1), (0, 2), (1, 2))
MIB = 1 << 20
VMEM = 56


def shifted(**steps):
    pairs = []
    for i, c in enumerate(np.ndindex(*SIZES)):
        d = dict(zip(AXES, c))
        for a, s in steps.items():
            d[a] = (d[a] + s) % SIZES[AXES.index(a)]
        pairs.append((i, int(np.ravel_multi_index(tuple(d[a] for a in AXES), SIZES))))
    return pairs


def send(v, **steps):
    return lax.ppermute(v, AXES, shifted(**steps))


ANY = pl.BlockSpec(memory_space=pl.ANY)


def after(v, *deps):
    return pl.pallas_call(
        lambda *refs: None,
        out_shape=jax.ShapeDtypeStruct(v.shape, v.dtype),
        in_specs=[ANY] * (1 + len(deps)),
        out_specs=ANY,
        input_output_aliases={0: 0},
        cost_estimate=pl.CostEstimate(flops=0, bytes_accessed=0, transcendentals=0),
        name="after",
    )(v, *deps)


def adamw(master, gradient, first_moment, second_moment):
    grad_float = gradient.astype(jnp.float32)
    first_new = beta_one * first_moment + (1.0 - beta_one) * grad_float
    second_new = beta_two * second_moment + (1.0 - beta_two) * grad_float * grad_float
    corr_one = 1.0 - beta_one**step_index
    corr_two = 1.0 - beta_two**step_index
    update = first_new * (1.0 / corr_one) / (jnp.sqrt(second_new * (1.0 / corr_two)) + adam_eps)
    return master - learn_rate * (update + decay_rate * master)


def params():
    return pltpu.CompilerParams(vmem_limit_bytes=VMEM * MIB)


def cost(flops, nbytes):
    return pl.CostEstimate(flops=int(flops) // 1000, bytes_accessed=int(nbytes) // 1000, transcendentals=0)


def up_kernel(w_ref, g_ref, m_ref, v_ref, o_ref, out_ref):
    new = adamw(w_ref[...], g_ref[...], m_ref[...], v_ref[...])
    o_ref[...] = new
    cast = new.astype(jnp.bfloat16)
    for n in range(16):
        out_ref[n] = cast[:, n * 128 : (n + 1) * 128]


def up_step(w, g, m, v):
    spec = pl.BlockSpec((32, 2048), lambda i: (0, i))
    return pl.pallas_call(
        up_kernel,
        out_shape=(
            jax.ShapeDtypeStruct((32, FF), jnp.float32),
            jax.ShapeDtypeStruct((16, 32, 1024), jnp.bfloat16),
        ),
        grid=(8,),
        in_specs=[spec] * 4,
        out_specs=(spec, pl.BlockSpec((16, 32, 128), lambda i: (0, 0, i))),
        compiler_params=params(),
        cost_estimate=cost(30 * 32 * FF, 20 * 32 * FF),
        name="adam_up",
    )(w, g, m, v)


SPLIT = ((0, 0), (0, 1), (1, 0), (1, 1))


def down_kernel(w_ref, g_ref, m_ref, v_ref, o_ref, *d_refs):
    new = adamw(w_ref[...], g_ref[...], m_ref[...], v_ref[...])
    o_ref[...] = new
    cast = new.astype(jnp.bfloat16)
    for t in range(8):
        for j in range(CHUNKS):
            piece = cast[:, t * 512 + j * 128 : t * 512 + (j + 1) * 128]
            d_refs[SPLIT[j][0]][SPLIT[j][1], :, t * 128 : (t + 1) * 128] = piece


def down_step(w, g, m, v):
    spec = pl.BlockSpec((32, D), lambda i: (i, 0))
    sizes = (2, 2)
    return pl.pallas_call(
        down_kernel,
        out_shape=(jax.ShapeDtypeStruct((128, D), jnp.float32),)
        + tuple(jax.ShapeDtypeStruct((n, 128, 1024), jnp.bfloat16) for n in sizes),
        grid=(4,),
        in_specs=[spec] * 4,
        out_specs=(spec,) + tuple(pl.BlockSpec((n, 32, 1024), lambda i: (0, i, 0)) for n in sizes),
        compiler_params=params(),
        cost_estimate=cost(30 * 128 * D, 20 * 128 * D),
        name="adam_down",
    )(w, g, m, v)


def both_ways(up, down):
    return send(up, z=1), send(down, z=-1)


def norm_kernel(a_ref, a1_ref, a2_ref, a3_ref, b_ref, g_ref, *refs):
    out = refs[-1]
    blocks = [a_ref[...], a1_ref[...], a2_ref[...], a3_ref[...]] + [b_ref[i] for i in range(4)]
    total = 0.0
    for block in blocks:
        f = block.astype(jnp.float32)
        total += jnp.sum(f * f, axis=-1, keepdims=True)
    scale = lax.rsqrt(total * (1.0 / D) + norm_eps)
    for n, block in enumerate(blocks):
        out[n] = (block.astype(jnp.float32) * scale * g_ref[n : n + 1]).astype(jnp.bfloat16)


def norm_of(feats_a, feats_b, gains, deps=()):
    rows = 160
    block = pl.BlockSpec((4, rows, 512), lambda i: (0, i, 0))
    return pl.pallas_call(
        norm_kernel,
        out_shape=jax.ShapeDtypeStruct((8, 640, 512), jnp.bfloat16),
        grid=(640 // rows,),
        in_specs=[pl.BlockSpec((rows, 512), lambda i: (i, 0))] * 4
        + [block, pl.BlockSpec((8, 512), lambda i: (0, 0))] + [ANY] * len(deps),
        out_specs=pl.BlockSpec((8, rows, 512), lambda i: (0, i, 0)),
        compiler_params=params(),
        cost_estimate=cost(8 * 640 * D, 10 * MIB),
        name="norm",
    )(*feats_a, feats_b, gains, *deps)


def silu(u):
    return u / (1.0 + jnp.exp(-u))


def first_kernel(s_ref, *refs):
    lhs, ws, acc = refs[:6], refs[6:12], refs[12]
    for k, (a, w) in enumerate(zip(lhs, ws)):
        term = jnp.dot(a[0], w[...], preferred_element_type=jnp.float32)
        if k == 0:
            acc[...] = term
        else:
            acc[...] += term


def last_kernel(s_ref, acc_ref, *refs):
    lhs, ws, out = refs[:2], refs[2:4], refs[4]
    for n in range(4):
        at = slice(n * 256, (n + 1) * 256)
        u = acc_ref[:, at]
        for a, w in zip(lhs, ws):
            u += jnp.dot(a[0], w[:, at], preferred_element_type=jnp.float32)
        out[:, at] = silu(u * D ** (-0.5)).astype(jnp.bfloat16)


def hidden_specs(places, ws):
    rows = 320
    lhs = [pl.BlockSpec((1, rows, 512), functools.partial(lambda k, i, s: (s[k], i, 0), k)) for k in places]
    return lhs, [pl.BlockSpec(w.shape, lambda i, s: (0, 0), pipeline_mode=pl.Buffered(1)) for w in ws]


def hidden_first(scalars, normed, ws):
    lhs, rhs = hidden_specs(range(6), ws)
    return pl.pallas_call(
        first_kernel,
        out_shape=jax.ShapeDtypeStruct((640, 1024), jnp.float32),
        grid_spec=pltpu.PrefetchScalarGridSpec(
            num_scalar_prefetch=1,
            grid=(2,),
            in_specs=lhs + rhs,
            out_specs=pl.BlockSpec((320, 1024), lambda i, s: (i, 0)),
        ),
        compiler_params=params(),
        cost_estimate=cost(2 * 640 * 1024 * 3072, 14 * MIB),
        name="hidden_first",
    )(scalars, *([normed] * 6), *ws)


def hidden_last(scalars, acc, normed, ws):
    lhs, rhs = hidden_specs((6, 7), ws)
    block = pl.BlockSpec((320, 1024), lambda i, s: (i, 0))
    return pl.pallas_call(
        last_kernel,
        out_shape=jax.ShapeDtypeStruct((640, 1024), jnp.bfloat16),
        grid_spec=pltpu.PrefetchScalarGridSpec(
            num_scalar_prefetch=1,
            grid=(2,),
            in_specs=[block] + lhs + rhs,
            out_specs=block,
        ),
        compiler_params=params(),
        cost_estimate=cost(2 * 640 * 1024 * 1024, 8 * MIB),
        name="hidden_last",
    )(scalars, acc, normed, normed, *ws)


def partial_kernel(s_ref, own_ref, sib_ref, w_ref, *refs):
    own_out, sib_out = refs[-2:]
    w = w_ref[:, 0].reshape(1024, 1024)
    for src, dst in ((sib_ref, sib_out), (own_ref, own_out)):
        term = jnp.dot(src[...], w, preferred_element_type=jnp.float32)
        term = (term * FF ** (-0.5)).astype(jnp.bfloat16)
        for xi in range(4):
            dst[s_ref[xi]] = term[:, xi * 256 : (xi + 1) * 256]


def partial_of(scalars, own, sib, w, j, deps):
    rows = 320
    block = pl.BlockSpec((rows, 1024), lambda i, s: (i, 0))
    out = pl.BlockSpec((4, rows, 256), lambda i, s: (0, i, 0))
    shape = jax.ShapeDtypeStruct((4, 640, 256), jnp.bfloat16)
    weights = pl.BlockSpec((8, 1, 128, 1024), lambda i, s: (0, j, 0, 0), pipeline_mode=pl.Buffered(1))
    return pl.pallas_call(
        partial_kernel,
        out_shape=(shape, shape),
        grid_spec=pltpu.PrefetchScalarGridSpec(
            num_scalar_prefetch=1,
            grid=(640 // rows,),
            in_specs=[block, block, weights] + [ANY] * len(deps),
            out_specs=(out, out),
        ),
        compiler_params=params(),
        cost_estimate=cost(4 * 640 * 1024 * 1024, 8 * MIB),
        name="partial",
    )(scalars, own, sib, w, *deps)


def slot_table():
    rows = []
    for ylo, z, yhi, x in np.ndindex(2, 4, 2, 4):
        qs = [(ylo ^ dy) * 4 + (z + dz) % 4 for dy, dz in ORDER]
        rows.append([(q // 2 - x) % 4 if q % 2 == yhi else 4 + q // 2 for q in qs])
    return np.array(rows, np.int32)


SLOTS = slot_table()


def body(
    tokens,
    norm_gain,
    up_master,
    up_gradient,
    up_first,
    up_second,
    down_master,
    down_gradient,
    down_first,
    down_second,
):
    ylo, z, core, x, yhi = (lax.axis_index(a) for a in AXES)

    tokens_b = send(tokens, yhi=1)
    near = [tokens, send(tokens, x=3), send(tokens, x=2), send(tokens, x=1)]

    up_updated, columns = up_step(up_master, up_gradient, up_first, up_second)
    down_updated, down_a, down_b = down_step(down_master, down_gradient, down_first, down_second)
    plane = ("ylo", "z")
    ws_a = lax.all_gather(down_a, plane, axis=0)

    u0 = lax.all_to_all(after(columns, down_a), ("core", "x", "yhi"), 0, 0, tiled=True).reshape(512, 1024)
    u1 = send(u0, ylo=1)
    low0, high0 = both_ways(u0, u0)
    feats_b = lax.all_gather(after(tokens_b, low0, high0, ws_a, *near[1:]), "x", axis=0)
    low1, high1 = both_ways(u1, u1)
    opp = (send(low0, z=1), send(high1, z=-1))
    ws_b = lax.all_gather(after(down_b, low1), plane, axis=0)

    gains = norm_gain.reshape(4, 2, 512)
    gain_a = lax.dynamic_index_in_dim(gains, yhi, 1, keepdims=False)
    gain_a = lax.dynamic_slice_in_dim(jnp.concatenate([gain_a, gain_a]), x, 4, 0)
    gain_b = lax.dynamic_index_in_dim(gains, 1 - yhi, 1, keepdims=False)
    gains = jnp.concatenate([gain_a, gain_b])
    near = [v.reshape(640, 512) for v in near]
    normed = norm_of(near, feats_b.reshape(4, 640, 512), gains, (low1, high1))
    normed_sib = send(normed, core=1)

    where = lax.dynamic_index_in_dim(jnp.asarray(SLOTS), ((ylo * 4 + z) * 2 + yhi) * 4 + x, 0, keepdims=False)
    ws_up = (u0, u1, low0, low1, high0, high1)
    firsts = [hidden_first(where, n, ws_up) for n in (normed, normed_sib)]
    hidden_own, hidden_sib = (hidden_last(where, f, n, opp) for f, n in zip(firsts, (normed, normed_sib)))

    pieces, parts, sums, reduced = [], [], [], []
    places = jnp.arange(4, dtype=jnp.int32)
    add = lambda a, b: (a.astype(jnp.float32) + b.astype(jnp.float32)).astype(jnp.bfloat16)
    for j in range(CHUNKS):
        direct = j != 2
        part, part_sib = partial_of(
            (places - x) % 4 if direct else places,
            hidden_own,
            hidden_sib,
            (ws_a, ws_b)[SPLIT[j][0]],
            SPLIT[j][1],
            parts[-1:] + sums[-2:-1] + (reduced if j == 2 else []),
        )
        parts.append(part_sib)
        part_sib = send(part_sib, core=1)
        if direct:
            terms = [add(part[d], part_sib[d]) for d in range(4)]
            sums.append(terms[1])
            terms = terms[:1] + [send(terms[d], x=d) for d in (1, 2, 3)]
            rows = sum(v.astype(jnp.float32) for v in terms).astype(jnp.bfloat16)
        else:
            both = add(part, part_sib)
            sums.append(both)
            rows = lax.psum_scatter(both, "x", scatter_dimension=0, tiled=True)[0]
        reduced.append(rows)
        keep = lax.dynamic_slice_in_dim(rows, yhi * 128, 128, 1)
        give = lax.dynamic_slice_in_dim(rows, (1 - yhi) * 128, 128, 1)
        pieces.append(add(keep, send(give, yhi=1)))
    decoded = jnp.concatenate(pieces, axis=1).reshape(2, 320, 512)
    return (up_updated, down_updated, decoded)


def solution(mesh):
    fine = Mesh(mesh.devices.reshape(SIZES), AXES)
    grp, tp = AXES[:3], AXES[3:]
    flat = P(AXES, None)
    in_specs = (P(None, grp, tp), P()) + (flat,) * 8
    out_specs = (flat, flat, P(None, grp, tp))
    return jax.shard_map(body, mesh=fine, in_specs=in_specs, out_specs=out_specs, check_vma=False)
```

```python
import functools

import jax
import jax.numpy as jnp
import numpy as np
from jax import lax
from jax.experimental import pallas as pl
from jax.experimental.pallas import tpu as pltpu
from jax.sharding import Mesh, PartitionSpec as P

learn_rate = 0.05
beta_one = 0.9
beta_two = 0.95
adam_eps = 1e-08
decay_rate = 0.1
step_index = 100
norm_eps = 1e-06

AXES = ("ylo", "z", "core", "x", "yhi")
SIZES = (2, 4, 2, 4, 2)
D, FF = 4096, 16384
CHUNKS = 4
ORDER = ((0, 0), (1, 0), (0, 3), (1, 3), (0, 1), (1, 1), (0, 2), (1, 2))
MIB = 1 << 20


def shifted(**steps):
    pairs = []
    for i, c in enumerate(np.ndindex(*SIZES)):
        d = dict(zip(AXES, c))
        for a, s in steps.items():
            d[a] = (d[a] + s) % SIZES[AXES.index(a)]
        pairs.append((i, int(np.ravel_multi_index(tuple(d[a] for a in AXES), SIZES))))
    return pairs


def send(v, **steps):
    return lax.ppermute(v, AXES, shifted(**steps))


ANY = pl.BlockSpec(memory_space=pl.ANY)


def after(v, *deps):
    return pl.pallas_call(
        lambda *refs: None,
        out_shape=jax.ShapeDtypeStruct(v.shape, v.dtype),
        in_specs=[ANY] * (1 + len(deps)),
        out_specs=ANY,
        input_output_aliases={0: 0},
        cost_estimate=pl.CostEstimate(flops=0, bytes_accessed=0, transcendentals=0),
        name="after",
    )(v, *deps)


def adamw(master, gradient, first_moment, second_moment):
    grad_float = gradient.astype(jnp.float32)
    first_new = beta_one * first_moment + (1.0 - beta_one) * grad_float
    second_new = beta_two * second_moment + (1.0 - beta_two) * grad_float * grad_float
    corr_one = 1.0 - beta_one**step_index
    corr_two = 1.0 - beta_two**step_index
    update = first_new * (1.0 / corr_one) / (jnp.sqrt(second_new * (1.0 / corr_two)) + adam_eps)
    return master - learn_rate * (update + decay_rate * master)


def params(limit=32):
    return pltpu.CompilerParams(vmem_limit_bytes=limit * MIB)


def cost(flops, nbytes):
    return pl.CostEstimate(flops=int(flops) // 1000, bytes_accessed=int(nbytes) // 1000, transcendentals=0)


def up_kernel(w_ref, g_ref, m_ref, v_ref, o_ref, out_ref):
    new = adamw(w_ref[...], g_ref[...], m_ref[...], v_ref[...])
    o_ref[...] = new
    cast = new.astype(jnp.bfloat16)
    for n in range(16):
        out_ref[n] = cast[:, n * 128 : (n + 1) * 128]


def up_step(w, g, m, v):
    spec = pl.BlockSpec((32, 2048), lambda i: (0, i))
    return pl.pallas_call(
        up_kernel,
        out_shape=(
            jax.ShapeDtypeStruct((32, FF), jnp.float32),
            jax.ShapeDtypeStruct((16, 32, 1024), jnp.bfloat16),
        ),
        grid=(8,),
        in_specs=[spec] * 4,
        out_specs=(spec, pl.BlockSpec((16, 32, 128), lambda i: (0, 0, i))),
        compiler_params=params(56),
        cost_estimate=cost(30 * 32 * FF, 20 * 32 * FF),
        name="adam_up",
    )(w, g, m, v)


SPLIT = ((0, 0), (0, 1), (1, 0), (1, 1))


def down_kernel(w_ref, g_ref, m_ref, v_ref, o_ref, *d_refs):
    new = adamw(w_ref[...], g_ref[...], m_ref[...], v_ref[...])
    o_ref[...] = new
    cast = new.astype(jnp.bfloat16)
    for t in range(8):
        for j in range(CHUNKS):
            piece = cast[:, t * 512 + j * 128 : t * 512 + (j + 1) * 128]
            d_refs[SPLIT[j][0]][SPLIT[j][1], :, t * 128 : (t + 1) * 128] = piece


def down_step(w, g, m, v):
    spec = pl.BlockSpec((32, D), lambda i: (i, 0))
    sizes = (2, 2)
    return pl.pallas_call(
        down_kernel,
        out_shape=(jax.ShapeDtypeStruct((128, D), jnp.float32),)
        + tuple(jax.ShapeDtypeStruct((n, 128, 1024), jnp.bfloat16) for n in sizes),
        grid=(4,),
        in_specs=[spec] * 4,
        out_specs=(spec,) + tuple(pl.BlockSpec((n, 32, 1024), lambda i: (0, i, 0)) for n in sizes),
        compiler_params=params(56),
        cost_estimate=cost(30 * 128 * D, 20 * 128 * D),
        name="adam_down",
    )(w, g, m, v)


def both_ways(up, down):
    return send(up, z=1), send(down, z=-1)


def norm_kernel(a_ref, b_ref, g_ref, *refs):
    out = refs[-1]
    blocks = [ref[i] for ref in (a_ref, b_ref) for i in range(4)]
    total = 0.0
    for block in blocks:
        f = block.astype(jnp.float32)
        total += jnp.sum(f * f, axis=-1, keepdims=True)
    scale = lax.rsqrt(total * (1.0 / D) + norm_eps)
    for n, block in enumerate(blocks):
        out[n] = (block.astype(jnp.float32) * scale * g_ref[n : n + 1]).astype(jnp.bfloat16)


def norm_of(feats_a, feats_b, gains, deps=()):
    rows = 160
    block = pl.BlockSpec((4, rows, 512), lambda i: (0, i, 0))
    return pl.pallas_call(
        norm_kernel,
        out_shape=jax.ShapeDtypeStruct((8, 640, 512), jnp.bfloat16),
        grid=(640 // rows,),
        in_specs=[block, block, pl.BlockSpec((8, 512), lambda i: (0, 0))] + [ANY] * len(deps),
        out_specs=pl.BlockSpec((8, rows, 512), lambda i: (0, i, 0)),
        compiler_params=params(),
        cost_estimate=cost(8 * 640 * D, 10 * MIB),
        name="norm",
    )(feats_a, feats_b, gains, *deps)


def silu(u):
    return u / (1.0 + jnp.exp(-u))


def first_kernel(s_ref, *refs):
    lhs, ws, acc = refs[:6], refs[6:12], refs[12]
    for k, (a, w) in enumerate(zip(lhs, ws)):
        term = jnp.dot(a[0], w[...], preferred_element_type=jnp.float32)
        if k == 0:
            acc[...] = term
        else:
            acc[...] += term


def last_kernel(s_ref, acc_ref, *refs):
    lhs, ws, out = refs[:2], refs[2:6], refs[6]
    for n in range(4):
        at = slice(n * 256, (n + 1) * 256)
        u = acc_ref[:, at]
        for k, w in enumerate(ws):
            a = lhs[k // 2][0, :, (k % 2) * 256 : (k % 2 + 1) * 256]
            u += jnp.dot(a, w[:, at], preferred_element_type=jnp.float32)
        h = silu(u * D ** (-0.5)).astype(jnp.bfloat16)
        for q in (2 * n, 2 * n + 1):
            to = pl.multiple_of(s_ref[8 + q] * 128, 128)
            out[:, pl.ds(to, 128)] = h[:, (q - 2 * n) * 128 : (q - 2 * n + 1) * 128]


def hidden_specs(places, ws):
    rows = 320
    lhs = [pl.BlockSpec((1, rows, 512), functools.partial(lambda k, i, s: (s[k], i, 0), k)) for k in places]
    return lhs, [pl.BlockSpec(w.shape, lambda i, s: (0, 0), pipeline_mode=pl.Buffered(1)) for w in ws]


def hidden_first(scalars, normed, ws):
    lhs, rhs = hidden_specs(range(6), ws)
    return pl.pallas_call(
        first_kernel,
        out_shape=jax.ShapeDtypeStruct((640, 1024), jnp.float32),
        grid_spec=pltpu.PrefetchScalarGridSpec(
            num_scalar_prefetch=1,
            grid=(2,),
            in_specs=lhs + rhs,
            out_specs=pl.BlockSpec((320, 1024), lambda i, s: (i, 0)),
        ),
        compiler_params=params(),
        cost_estimate=cost(2 * 640 * 1024 * 3072, 14 * MIB),
        name="hidden_first",
    )(scalars, *([normed] * 6), *ws)


def hidden_last(scalars, acc, normed, ws):
    lhs, rhs = hidden_specs((6, 7), ws)
    block = pl.BlockSpec((320, 1024), lambda i, s: (i, 0))
    return pl.pallas_call(
        last_kernel,
        out_shape=jax.ShapeDtypeStruct((640, 1024), jnp.bfloat16),
        grid_spec=pltpu.PrefetchScalarGridSpec(
            num_scalar_prefetch=1,
            grid=(2,),
            in_specs=[block] + lhs + rhs,
            out_specs=block,
        ),
        compiler_params=params(),
        cost_estimate=cost(2 * 640 * 1024 * 1024, 8 * MIB),
        name="hidden_last",
    )(scalars, acc, normed, normed, *ws)


def partial_kernel(s_ref, own_ref, sib_ref, *refs):
    ws, (own_out, sib_out, w_ref) = refs[:5], refs[-3:]

    @pl.when(pl.program_id(0) == 0)
    def _():
        at = 0
        for w in ws:
            for part in [w[0, 0], w[1, 0]] if len(w.shape) == 4 else [w[0]]:
                w_ref[at : at + 128] = part
                at += 128

    for src, dst in ((sib_ref, sib_out), (own_ref, own_out)):
        term = jnp.dot(src[...], w_ref[...], preferred_element_type=jnp.float32)
        term = (term * FF ** (-0.5)).astype(jnp.bfloat16)
        for xi in range(4):
            dst[s_ref[xi]] = term[:, xi * 256 : (xi + 1) * 256]


def partial_of(scalars, own, sib, ws, j, deps):
    rows = 320
    block = pl.BlockSpec((rows, 1024), lambda i, s: (i, 0))
    out = pl.BlockSpec((4, rows, 256), lambda i, s: (0, i, 0))
    shape = jax.ShapeDtypeStruct((4, 640, 256), jnp.bfloat16)
    two = pl.BlockSpec((2, 1, 128, 1024), lambda i, s: (0, j, 0, 0), pipeline_mode=pl.Buffered(1))
    one = pl.BlockSpec((1, 128, 1024), lambda i, s: (j, 0, 0), pipeline_mode=pl.Buffered(1))
    return pl.pallas_call(
        partial_kernel,
        out_shape=(shape, shape),
        grid_spec=pltpu.PrefetchScalarGridSpec(
            num_scalar_prefetch=1,
            grid=(640 // rows,),
            in_specs=[block, block, two, two, two, one, one] + [ANY] * len(deps),
            out_specs=(out, out),
            scratch_shapes=[pltpu.VMEM((1024, 1024), jnp.bfloat16)],
        ),
        compiler_params=params(),
        cost_estimate=cost(4 * 640 * 1024 * 1024, 8 * MIB),
        name="partial",
    )(scalars, own, sib, *ws, *deps)


def slot_table():
    rows = []
    for ylo, z, yhi in np.ndindex(2, 4, 2):
        qs = [(ylo ^ dy) * 4 + (z + dz) % 4 for dy, dz in ORDER]
        rows.append([((q % 2) ^ yhi) * 4 + q // 2 for q in qs] + [qs.index(q) for q in range(8)])
    return np.array(rows, np.int32)


SLOTS = slot_table()


def body(
    tokens,
    norm_gain,
    up_master,
    up_gradient,
    up_first,
    up_second,
    down_master,
    down_gradient,
    down_first,
    down_second,
):
    ylo, z, core, x, yhi = (lax.axis_index(a) for a in AXES)

    tokens_b = send(tokens, yhi=1)
    feats_a = lax.all_gather(tokens, "x", axis=0)

    up_updated, columns = up_step(up_master, up_gradient, up_first, up_second)
    down_updated, down_a, down_b = down_step(down_master, down_gradient, down_first, down_second)

    st_a = jnp.stack([down_a, send(down_a, ylo=1)])
    low_a, high_a = both_ways(st_a, st_a)
    u0 = lax.all_to_all(after(columns, down_a), ("core", "x", "yhi"), 0, 0, tiled=True).reshape(512, 1024)
    feats_b = lax.all_gather(after(tokens_b, u0), "x", axis=0)
    opp_a = both_ways(low_a[0], high_a[1])
    ws_a = (st_a, low_a, high_a, *opp_a)

    u1 = send(u0, ylo=1)
    low0, high0 = both_ways(u0, u0)
    down_b = after(down_b, u1)
    ylo_b = send(down_b, ylo=1)
    low1, high1 = both_ways(u1, u1)
    opp0 = both_ways(after(low0[:256], u1, *opp_a), high0[256:])
    opp1 = both_ways(low1[:256], high1[256:])
    st_b = after(jnp.stack([down_b, ylo_b]), low1)
    low_b, high_b = both_ways(st_b, st_b)
    ws_b = (st_b, low_b, high_b, *both_ways(low_b[0], high_b[1]))

    gains = norm_gain.reshape(4, 2, 512)
    gains = jnp.concatenate([lax.dynamic_index_in_dim(gains, k, 1, keepdims=False) for k in (yhi, 1 - yhi)])
    feats_a, feats_b = feats_a.reshape(4, 640, 512), feats_b.reshape(4, 640, 512)
    normed = norm_of(feats_a, feats_b, gains, (low1, high1, *opp0, ylo_b))
    normed_sib = send(normed, core=1)

    where = lax.dynamic_index_in_dim(jnp.asarray(SLOTS), (ylo * 4 + z) * 2 + yhi, 0, keepdims=False)
    ws_up = (u0, u1, low0, low1, high0, high1)
    firsts = [hidden_first(where, n, ws_up) for n in (normed, normed_sib)]
    hidden_own, hidden_sib = (
        hidden_last(where, f, n, opp0 + opp1) for f, n in zip(firsts, (normed, normed_sib))
    )

    pieces, parts, sums, reduced = [], [], [], []
    places = jnp.arange(4, dtype=jnp.int32)
    add = lambda a, b: (a.astype(jnp.float32) + b.astype(jnp.float32)).astype(jnp.bfloat16)
    for j in range(CHUNKS):
        direct = j % 2 == 1
        part, part_sib = partial_of(
            (places - x) % 4 if direct else places,
            hidden_own,
            hidden_sib,
            (ws_a, ws_b)[SPLIT[j][0]],
            SPLIT[j][1],
            ([], parts + [low_b, high_b], sums + reduced[1:], parts[2:] + reduced[:2])[j],
        )
        parts.append(part_sib)
        part_sib = send(part_sib, core=1)
        if direct:
            terms = [add(part[d], part_sib[d]) for d in range(4)]
            sums.append(terms[1])
            terms = terms[:1] + [send(terms[d], x=d) for d in (1, 2, 3)]
            rows = sum(v.astype(jnp.float32) for v in terms).astype(jnp.bfloat16)
        else:
            both = add(part, part_sib)
            sums.append(both)
            rows = lax.psum_scatter(both, "x", scatter_dimension=0, tiled=True)[0]
        reduced.append(rows)
        keep = lax.dynamic_slice_in_dim(rows, yhi * 128, 128, 1)
        give = lax.dynamic_slice_in_dim(rows, (1 - yhi) * 128, 128, 1)
        pieces.append(add(keep, send(give, yhi=1)))
    decoded = jnp.concatenate(pieces, axis=1).reshape(2, 320, 512)
    return (up_updated, down_updated, decoded)


def solution(mesh):
    fine = Mesh(mesh.devices.reshape(SIZES), AXES)
    grp, tp = AXES[:3], AXES[3:]
    flat = P(AXES, None)
    in_specs = (P(None, grp, tp), P()) + (flat,) * 8
    out_specs = (flat, flat, P(None, grp, tp))
    return jax.shard_map(body, mesh=fine, in_specs=in_specs, out_specs=out_specs, check_vma=False)
```

```python
import functools

import jax
import jax.numpy as jnp
import numpy as np
from jax import lax
from jax.experimental import pallas as pl
from jax.experimental.pallas import tpu as pltpu
from jax.sharding import Mesh, PartitionSpec as P

learn_rate = 0.05
beta_one = 0.9
beta_two = 0.95
adam_eps = 1e-08
decay_rate = 0.1
step_index = 100
norm_eps = 1e-06

AXES = ("ylo", "z", "core", "x", "yhi")
SIZES = (2, 4, 2, 4, 2)
D, FF = 4096, 16384
CHUNKS = 4
ORDER = ((0, 0), (1, 0), (0, 3), (1, 3), (0, 1), (1, 1), (0, 2), (1, 2))
MIB = 1 << 20


def shifted(**steps):
    pairs = []
    for i, c in enumerate(np.ndindex(*SIZES)):
        d = dict(zip(AXES, c))
        for a, s in steps.items():
            d[a] = (d[a] + s) % SIZES[AXES.index(a)]
        pairs.append((i, int(np.ravel_multi_index(tuple(d[a] for a in AXES), SIZES))))
    return pairs


def send(v, **steps):
    return lax.ppermute(v, AXES, shifted(**steps))


ANY = pl.BlockSpec(memory_space=pl.ANY)


def after(v, *deps):
    return pl.pallas_call(
        lambda *refs: None,
        out_shape=jax.ShapeDtypeStruct(v.shape, v.dtype),
        in_specs=[ANY] * (1 + len(deps)),
        out_specs=ANY,
        input_output_aliases={0: 0},
        cost_estimate=pl.CostEstimate(flops=0, bytes_accessed=0, transcendentals=0),
        name="after",
    )(v, *deps)


def adamw(master, gradient, first_moment, second_moment):
    grad_float = gradient.astype(jnp.float32)
    first_new = beta_one * first_moment + (1.0 - beta_one) * grad_float
    second_new = beta_two * second_moment + (1.0 - beta_two) * grad_float * grad_float
    corr_one = 1.0 - beta_one**step_index
    corr_two = 1.0 - beta_two**step_index
    update = first_new * (1.0 / corr_one) / (jnp.sqrt(second_new * (1.0 / corr_two)) + adam_eps)
    return master - learn_rate * (update + decay_rate * master)


def params(limit=32):
    return pltpu.CompilerParams(vmem_limit_bytes=limit * MIB)


def cost(flops, nbytes):
    return pl.CostEstimate(flops=int(flops) // 1000, bytes_accessed=int(nbytes) // 1000, transcendentals=0)


def up_kernel(w_ref, g_ref, m_ref, v_ref, dep_ref, o_ref, out_ref):
    new = adamw(w_ref[...], g_ref[...], m_ref[...], v_ref[...])
    o_ref[...] = new
    cast = new.astype(jnp.bfloat16)
    for n in range(16):
        out_ref[n] = cast[:, n * 128 : (n + 1) * 128]


def up_step(w, g, m, v, dep):
    spec = pl.BlockSpec((32, 2048), lambda i: (0, i))
    return pl.pallas_call(
        up_kernel,
        out_shape=(
            jax.ShapeDtypeStruct((32, FF), jnp.float32),
            jax.ShapeDtypeStruct((16, 32, 1024), jnp.bfloat16),
        ),
        grid=(8,),
        in_specs=[spec] * 4 + [ANY],
        out_specs=(spec, pl.BlockSpec((16, 32, 128), lambda i: (0, 0, i))),
        compiler_params=params(56),
        cost_estimate=cost(30 * 32 * FF, 20 * 32 * FF),
        name="adam_up",
    )(w, g, m, v, dep)


def down_kernel(w_ref, g_ref, m_ref, v_ref, *refs):
    o_ref, d_ref = refs[-2:]
    new = adamw(w_ref[...], g_ref[...], m_ref[...], v_ref[...])
    o_ref[...] = new
    cast = new.astype(jnp.bfloat16)
    d_ref[0] = cast[:, :128]
    d_ref[1] = cast[:, 128:]


def down_step(half, args, done=(), deps=()):
    spec = pl.BlockSpec((128, 256), lambda i: (0, 2 * i + half))
    return pl.pallas_call(
        down_kernel,
        out_shape=(
            jax.ShapeDtypeStruct((128, D), jnp.float32),
            jax.ShapeDtypeStruct((2, 128, 1024), jnp.bfloat16),
        ),
        grid=(8,),
        in_specs=[spec] * 4 + [ANY] * (len(done) + len(deps)),
        out_specs=(spec, pl.BlockSpec((2, 128, 128), lambda i: (0, 0, i))),
        input_output_aliases={4: 0} if done else {},
        compiler_params=params(56),
        cost_estimate=cost(15 * 128 * D, 10 * 128 * D),
        name="adam_down",
    )(*args, *done, *deps)


def both_ways(up, down):
    return send(up, z=1), send(down, z=-1)


def norm_kernel(a_ref, b_ref, g_ref, *refs):
    out = refs[-1]
    blocks = [ref[i] for ref in (a_ref, b_ref) for i in range(4)]
    total = 0.0
    for block in blocks:
        f = block.astype(jnp.float32)
        total += jnp.sum(f * f, axis=-1, keepdims=True)
    scale = lax.rsqrt(total * (1.0 / D) + norm_eps)
    for n, block in enumerate(blocks):
        out[n] = (block.astype(jnp.float32) * scale * g_ref[n : n + 1]).astype(jnp.bfloat16)


def norm_of(feats_a, feats_b, gains, deps=()):
    rows = 160
    block = pl.BlockSpec((4, rows, 512), lambda i: (0, i, 0))
    return pl.pallas_call(
        norm_kernel,
        out_shape=jax.ShapeDtypeStruct((8, 640, 512), jnp.bfloat16),
        grid=(640 // rows,),
        in_specs=[block, block, pl.BlockSpec((8, 512), lambda i: (0, 0))] + [ANY] * len(deps),
        out_specs=pl.BlockSpec((8, rows, 512), lambda i: (0, i, 0)),
        compiler_params=params(),
        cost_estimate=cost(8 * 640 * D, 10 * MIB),
        name="norm",
    )(feats_a, feats_b, gains, *deps)


def silu(u):
    return u / (1.0 + jnp.exp(-u))


def first_kernel(s_ref, *refs):
    lhs, ws, acc = refs[:6], refs[6:12], refs[12]
    for k, (a, w) in enumerate(zip(lhs, ws)):
        term = jnp.dot(a[0], w[...], preferred_element_type=jnp.float32)
        if k == 0:
            acc[...] = term
        else:
            acc[...] += term


def last_kernel(s_ref, acc_ref, *refs):
    lhs, ws, out = refs[:2], refs[2:6], refs[-1]
    for n in range(4):
        at = slice(n * 256, (n + 1) * 256)
        u = acc_ref[:, at]
        for k, w in enumerate(ws):
            a = lhs[k // 2][0, :, (k % 2) * 256 : (k % 2 + 1) * 256]
            u += jnp.dot(a, w[:, at], preferred_element_type=jnp.float32)
        h = silu(u * D ** (-0.5)).astype(jnp.bfloat16)
        for q in (2 * n, 2 * n + 1):
            to = pl.multiple_of(s_ref[8 + q] * 128, 128)
            out[:, pl.ds(to, 128)] = h[:, (q - 2 * n) * 128 : (q - 2 * n + 1) * 128]


def hidden_specs(places, ws):
    rows = 320
    lhs = [pl.BlockSpec((1, rows, 512), functools.partial(lambda k, i, s: (s[k], i, 0), k)) for k in places]
    return lhs, [pl.BlockSpec(w.shape, lambda i, s: (0, 0), pipeline_mode=pl.Buffered(1)) for w in ws]


def hidden_first(scalars, normed, ws):
    lhs, rhs = hidden_specs(range(6), ws)
    return pl.pallas_call(
        first_kernel,
        out_shape=jax.ShapeDtypeStruct((640, 1024), jnp.float32),
        grid_spec=pltpu.PrefetchScalarGridSpec(
            num_scalar_prefetch=1,
            grid=(2,),
            in_specs=lhs + rhs,
            out_specs=pl.BlockSpec((320, 1024), lambda i, s: (i, 0)),
        ),
        compiler_params=params(),
        cost_estimate=cost(2 * 640 * 1024 * 3072, 14 * MIB),
        name="hidden_first",
    )(scalars, *([normed] * 6), *ws)


def hidden_last(scalars, acc, normed, ws, deps):
    lhs, rhs = hidden_specs((6, 7), ws)
    block = pl.BlockSpec((320, 1024), lambda i, s: (i, 0))
    return pl.pallas_call(
        last_kernel,
        out_shape=jax.ShapeDtypeStruct((640, 1024), jnp.bfloat16),
        grid_spec=pltpu.PrefetchScalarGridSpec(
            num_scalar_prefetch=1,
            grid=(2,),
            in_specs=[block] + lhs + rhs + [ANY] * len(deps),
            out_specs=block,
        ),
        compiler_params=params(),
        cost_estimate=cost(2 * 640 * 1024 * 1024, 8 * MIB),
        name="hidden_last",
    )(scalars, acc, normed, normed, *ws, *deps)


def partial_kernel(s_ref, own_ref, sib_ref, *refs):
    ws, (own_out, sib_out, w_ref) = refs[:5], refs[-3:]

    @pl.when(pl.program_id(0) == 0)
    def _():
        at = 0
        for w in ws:
            for part in [w[0, 0], w[1, 0]] if len(w.shape) == 4 else [w[0]]:
                w_ref[at : at + 128] = part
                at += 128

    for src, dst in ((sib_ref, sib_out), (own_ref, own_out)):
        term = jnp.dot(src[...], w_ref[...], preferred_element_type=jnp.float32)
        term = (term * FF ** (-0.5)).astype(jnp.bfloat16)
        for xi in range(4):
            dst[s_ref[xi]] = term[:, xi * 256 : (xi + 1) * 256]


def partial_of(scalars, own, sib, ws, j, deps):
    rows = 320
    block = pl.BlockSpec((rows, 1024), lambda i, s: (i, 0))
    out = pl.BlockSpec((4, rows, 256), lambda i, s: (0, i, 0))
    shape = jax.ShapeDtypeStruct((4, 640, 256), jnp.bfloat16)
    two = pl.BlockSpec((2, 1, 128, 1024), lambda i, s: (0, j, 0, 0), pipeline_mode=pl.Buffered(1))
    one = pl.BlockSpec((1, 128, 1024), lambda i, s: (j, 0, 0), pipeline_mode=pl.Buffered(1))
    return pl.pallas_call(
        partial_kernel,
        out_shape=(shape, shape),
        grid_spec=pltpu.PrefetchScalarGridSpec(
            num_scalar_prefetch=1,
            grid=(640 // rows,),
            in_specs=[block, block, two, two, two, one, one] + [ANY] * len(deps),
            out_specs=(out, out),
            scratch_shapes=[pltpu.VMEM((1024, 1024), jnp.bfloat16)],
        ),
        compiler_params=params(56),
        cost_estimate=cost(4 * 640 * 1024 * 1024, 8 * MIB),
        name="partial",
    )(scalars, own, sib, *ws, *deps)


def slot_table():
    rows = []
    for ylo, z, yhi in np.ndindex(2, 4, 2):
        qs = [(ylo ^ dy) * 4 + (z + dz) % 4 for dy, dz in ORDER]
        rows.append([((q % 2) ^ yhi) * 4 + q // 2 for q in qs] + [qs.index(q) for q in range(8)])
    return np.array(rows, np.int32)


SLOTS = slot_table()


def body(
    tokens,
    norm_gain,
    up_master,
    up_gradient,
    up_first,
    up_second,
    down_master,
    down_gradient,
    down_first,
    down_second,
):
    ylo, z, core, x, yhi = (lax.axis_index(a) for a in AXES)

    tokens_b = send(tokens, yhi=1)
    feats_a = lax.all_gather(tokens, "x", axis=0)

    down_args = (down_master, down_gradient, down_first, down_second)
    down_half, down_a = down_step(0, down_args)
    ylo_a = send(down_a, ylo=1)
    up_updated, columns = up_step(up_master, up_gradient, up_first, up_second, down_a)
    down_updated, down_b = down_step(1, down_args, (down_half,), (ylo_a,))

    st_a = jnp.stack([down_a, ylo_a])
    low_a, high_a = both_ways(st_a, st_a)
    u0 = lax.all_to_all(columns, ("core", "x", "yhi"), 0, 0, tiled=True).reshape(512, 1024)
    u0 = after(u0, down_b, low_a, high_a)
    feats_b = lax.all_gather(after(tokens_b, u0), "x", axis=0)
    opp_a = both_ways(low_a[0], high_a[1])
    ws_a = (st_a, low_a, high_a, *opp_a)

    u1 = send(u0, ylo=1)
    low0, high0 = both_ways(u0, u0)
    down_b = after(down_b, u1)
    ylo_b = send(down_b, ylo=1)
    low1, high1 = both_ways(u1, u1)
    opp0 = both_ways(after(low0[:256], u1, *opp_a), high0[256:])
    opp1 = both_ways(low1[:256], high1[256:])
    st_b = after(jnp.stack([down_b, ylo_b]), low1)
    low_b, high_b = both_ways(st_b, st_b)

    gains = norm_gain.reshape(4, 2, 512)
    gains = jnp.concatenate([lax.dynamic_index_in_dim(gains, k, 1, keepdims=False) for k in (yhi, 1 - yhi)])
    feats_a, feats_b = feats_a.reshape(4, 640, 512), feats_b.reshape(4, 640, 512)
    normed = norm_of(feats_a, feats_b, gains, (low1, high1, *opp0, ylo_b))
    normed_sib = send(normed, core=1)

    where = lax.dynamic_index_in_dim(jnp.asarray(SLOTS), (ylo * 4 + z) * 2 + yhi, 0, keepdims=False)
    ws_up = (u0, u1, low0, low1, high0, high1)
    firsts = [hidden_first(where, n, ws_up) for n in (normed, normed_sib)]
    hidden_own, hidden_sib = (
        hidden_last(where, f, n, opp0 + opp1, firsts) for f, n in zip(firsts, (normed, normed_sib))
    )

    pieces, sums, reduced = [], [], []
    places = jnp.arange(4, dtype=jnp.int32)
    add = lambda a, b: (a.astype(jnp.float32) + b.astype(jnp.float32)).astype(jnp.bfloat16)
    for j in range(CHUNKS):
        direct = j in (0, 3)
        if j == 2:
            up, down = after(low_b[0], *reduced), after(high_b[1], *reduced)
            ws_b = (st_b, low_b, high_b, *both_ways(up, down))
        part, part_sib = partial_of(
            (places - x) % 4 if direct else places,
            hidden_own,
            hidden_sib,
            ws_a if j < 2 else ws_b,
            j % 2,
            sums[-1:],
        )
        part_sib = send(part_sib, core=1)
        if direct:
            terms = [add(part[d], part_sib[d]) for d in range(4)]
            sums.append(terms[1])
            terms = terms[:1] + [send(terms[d], x=d) for d in (1, 2, 3)]
            rows = sum(v.astype(jnp.float32) for v in terms).astype(jnp.bfloat16)
            reduced.append(rows)
        else:
            both = add(part, part_sib)
            sums.append(both)
            rows = lax.psum_scatter(both, "x", scatter_dimension=0, tiled=True)[0]
        keep = lax.dynamic_slice_in_dim(rows, yhi * 128, 128, 1)
        give = lax.dynamic_slice_in_dim(rows, (1 - yhi) * 128, 128, 1)
        pieces.append(add(keep, send(give, yhi=1)))
    decoded = jnp.concatenate(pieces, axis=1).reshape(2, 320, 512)
    return (up_updated, down_updated, decoded)


def solution(mesh):
    fine = Mesh(mesh.devices.reshape(SIZES), AXES)
    grp, tp = AXES[:3], AXES[3:]
    flat = P(AXES, None)
    in_specs = (P(None, grp, tp), P()) + (flat,) * 8
    out_specs = (flat, flat, P(None, grp, tp))
    return jax.shard_map(body, mesh=fine, in_specs=in_specs, out_specs=out_specs, check_vma=False)
```

```python
import functools

import jax
import jax.numpy as jnp
import numpy as np
from jax import lax
from jax.experimental import pallas as pl
from jax.experimental.pallas import tpu as pltpu
from jax.sharding import Mesh, PartitionSpec as P

learn_rate = 0.05
beta_one = 0.9
beta_two = 0.95
adam_eps = 1e-08
decay_rate = 0.1
step_index = 100
norm_eps = 1e-06

AXES = ("ylo", "z", "core", "x", "yhi")
SIZES = (2, 4, 2, 4, 2)
D, FF = 4096, 16384
CHUNKS = 4
ORDER = ((0, 0), (1, 0), (0, 3), (1, 3), (0, 1), (1, 1), (0, 2), (1, 2))
MIB = 1 << 20


def shifted(**steps):
    pairs = []
    for i, c in enumerate(np.ndindex(*SIZES)):
        d = dict(zip(AXES, c))
        for a, s in steps.items():
            d[a] = (d[a] + s) % SIZES[AXES.index(a)]
        pairs.append((i, int(np.ravel_multi_index(tuple(d[a] for a in AXES), SIZES))))
    return pairs


def send(v, **steps):
    return lax.ppermute(v, AXES, shifted(**steps))


ANY = pl.BlockSpec(memory_space=pl.ANY)


def after(v, *deps):
    return pl.pallas_call(
        lambda *refs: None,
        out_shape=jax.ShapeDtypeStruct(v.shape, v.dtype),
        in_specs=[ANY] * (1 + len(deps)),
        out_specs=ANY,
        input_output_aliases={0: 0},
        cost_estimate=pl.CostEstimate(flops=0, bytes_accessed=0, transcendentals=0),
        name="after",
    )(v, *deps)


def adamw(master, gradient, first_moment, second_moment):
    grad_float = gradient.astype(jnp.float32)
    first_new = beta_one * first_moment + (1.0 - beta_one) * grad_float
    second_new = beta_two * second_moment + (1.0 - beta_two) * grad_float * grad_float
    corr_one = 1.0 - beta_one**step_index
    corr_two = 1.0 - beta_two**step_index
    update = first_new * (1.0 / corr_one) / (jnp.sqrt(second_new * (1.0 / corr_two)) + adam_eps)
    return master - learn_rate * (update + decay_rate * master)


def params(limit=32):
    return pltpu.CompilerParams(vmem_limit_bytes=limit * MIB)


def cost(flops, nbytes):
    return pl.CostEstimate(flops=int(flops) // 1000, bytes_accessed=int(nbytes) // 1000, transcendentals=0)


def up_kernel(w_ref, g_ref, m_ref, v_ref, dep_ref, o_ref, out_ref):
    new = adamw(w_ref[...], g_ref[...], m_ref[...], v_ref[...])
    o_ref[...] = new
    cast = new.astype(jnp.bfloat16)
    for n in range(16):
        out_ref[n] = cast[:, n * 128 : (n + 1) * 128]


def up_step(w, g, m, v, dep):
    spec = pl.BlockSpec((32, 2048), lambda i: (0, i))
    return pl.pallas_call(
        up_kernel,
        out_shape=(
            jax.ShapeDtypeStruct((32, FF), jnp.float32),
            jax.ShapeDtypeStruct((16, 32, 1024), jnp.bfloat16),
        ),
        grid=(8,),
        in_specs=[spec] * 4 + [ANY],
        out_specs=(spec, pl.BlockSpec((16, 32, 128), lambda i: (0, 0, i))),
        compiler_params=params(56),
        cost_estimate=cost(30 * 32 * FF, 20 * 32 * FF),
        name="adam_up",
    )(w, g, m, v, dep)


def down_kernel(w_ref, g_ref, m_ref, v_ref, *refs):
    o_ref, d_ref = refs[-2:]
    new = adamw(w_ref[...], g_ref[...], m_ref[...], v_ref[...])
    o_ref[...] = new
    cast = new.astype(jnp.bfloat16)
    d_ref[0] = cast[:, :128]
    d_ref[1] = cast[:, 128:]


def down_step(half, args, done=(), deps=()):
    spec = pl.BlockSpec((128, 256), lambda i: (0, 2 * i + half))
    return pl.pallas_call(
        down_kernel,
        out_shape=(
            jax.ShapeDtypeStruct((128, D), jnp.float32),
            jax.ShapeDtypeStruct((2, 128, 1024), jnp.bfloat16),
        ),
        grid=(8,),
        in_specs=[spec] * 4 + [ANY] * (len(done) + len(deps)),
        out_specs=(spec, pl.BlockSpec((2, 128, 128), lambda i: (0, 0, i))),
        input_output_aliases={4: 0} if done else {},
        compiler_params=params(56),
        cost_estimate=cost(15 * 128 * D, 10 * 128 * D),
        name="adam_down",
    )(*args, *done, *deps)


def both_ways(up, down):
    return send(up, z=1), send(down, z=-1)


def norm_kernel(a_ref, b_ref, g_ref, *refs):
    out = refs[-1]
    blocks = [ref[i] for ref in (a_ref, b_ref) for i in range(4)]
    total = 0.0
    for block in blocks:
        f = block.astype(jnp.float32)
        total += jnp.sum(f * f, axis=-1, keepdims=True)
    scale = lax.rsqrt(total * (1.0 / D) + norm_eps)
    for n, block in enumerate(blocks):
        out[n] = (block.astype(jnp.float32) * scale * g_ref[n : n + 1]).astype(jnp.bfloat16)


def norm_of(feats_a, feats_b, gains, deps=()):
    rows = 160
    block = pl.BlockSpec((4, rows, 512), lambda i: (0, i, 0))
    return pl.pallas_call(
        norm_kernel,
        out_shape=jax.ShapeDtypeStruct((8, 640, 512), jnp.bfloat16),
        grid=(640 // rows,),
        in_specs=[block, block, pl.BlockSpec((8, 512), lambda i: (0, 0))] + [ANY] * len(deps),
        out_specs=pl.BlockSpec((8, rows, 512), lambda i: (0, i, 0)),
        compiler_params=params(),
        cost_estimate=cost(8 * 640 * D, 10 * MIB),
        name="norm",
    )(feats_a, feats_b, gains, *deps)


def silu(u):
    return u / (1.0 + jnp.exp(-u))


def first_kernel(s_ref, *refs):
    lhs, ws, acc = refs[:6], refs[6:12], refs[12]
    for k, (a, w) in enumerate(zip(lhs, ws)):
        term = jnp.dot(a[0], w[...], preferred_element_type=jnp.float32)
        if k == 0:
            acc[...] = term
        else:
            acc[...] += term


def last_kernel(s_ref, acc_ref, *refs):
    lhs, ws, out = refs[:2], refs[2:6], refs[-1]
    for n in range(4):
        at = slice(n * 256, (n + 1) * 256)
        u = acc_ref[:, at]
        for k, w in enumerate(ws):
            a = lhs[k // 2][0, :, (k % 2) * 256 : (k % 2 + 1) * 256]
            u += jnp.dot(a, w[:, at], preferred_element_type=jnp.float32)
        h = silu(u * D ** (-0.5)).astype(jnp.bfloat16)
        for q in (2 * n, 2 * n + 1):
            to = pl.multiple_of(s_ref[8 + q] * 128, 128)
            out[:, pl.ds(to, 128)] = h[:, (q - 2 * n) * 128 : (q - 2 * n + 1) * 128]


def hidden_specs(places, ws):
    rows = 320
    lhs = [pl.BlockSpec((1, rows, 512), functools.partial(lambda k, i, s: (s[k], i, 0), k)) for k in places]
    return lhs, [pl.BlockSpec(w.shape, lambda i, s: (0, 0), pipeline_mode=pl.Buffered(1)) for w in ws]


def hidden_first(scalars, normed, ws):
    lhs, rhs = hidden_specs(range(6), ws)
    return pl.pallas_call(
        first_kernel,
        out_shape=jax.ShapeDtypeStruct((640, 1024), jnp.float32),
        grid_spec=pltpu.PrefetchScalarGridSpec(
            num_scalar_prefetch=1,
            grid=(2,),
            in_specs=lhs + rhs,
            out_specs=pl.BlockSpec((320, 1024), lambda i, s: (i, 0)),
        ),
        compiler_params=params(),
        cost_estimate=cost(2 * 640 * 1024 * 3072, 14 * MIB),
        name="hidden_first",
    )(scalars, *([normed] * 6), *ws)


def hidden_last(scalars, acc, normed, ws, deps):
    lhs, rhs = hidden_specs((6, 7), ws)
    block = pl.BlockSpec((320, 1024), lambda i, s: (i, 0))
    return pl.pallas_call(
        last_kernel,
        out_shape=jax.ShapeDtypeStruct((640, 1024), jnp.bfloat16),
        grid_spec=pltpu.PrefetchScalarGridSpec(
            num_scalar_prefetch=1,
            grid=(2,),
            in_specs=[block] + lhs + rhs + [ANY] * len(deps),
            out_specs=block,
        ),
        compiler_params=params(),
        cost_estimate=cost(2 * 640 * 1024 * 1024, 8 * MIB),
        name="hidden_last",
    )(scalars, acc, normed, normed, *ws, *deps)


def partial_kernel(s_ref, own_ref, sib_ref, *refs):
    ws, (own_out, sib_out, w_ref) = refs[:5], refs[-3:]

    @pl.when(pl.program_id(0) == 0)
    def _():
        at = 0
        for w in ws:
            for part in [w[0, 0], w[1, 0]] if len(w.shape) == 4 else [w[0]]:
                w_ref[at : at + 128] = part
                at += 128

    for src, dst in ((sib_ref, sib_out), (own_ref, own_out)):
        term = jnp.dot(src[...], w_ref[...], preferred_element_type=jnp.float32)
        term = (term * FF ** (-0.5)).astype(jnp.bfloat16)
        for xi in range(4):
            dst[s_ref[xi]] = term[:, xi * 256 : (xi + 1) * 256]


def partial_of(scalars, own, sib, ws, j, deps):
    rows = 320
    block = pl.BlockSpec((rows, 1024), lambda i, s: (i, 0))
    out = pl.BlockSpec((4, rows, 256), lambda i, s: (0, i, 0))
    shape = jax.ShapeDtypeStruct((4, 640, 256), jnp.bfloat16)
    two = pl.BlockSpec((2, 1, 128, 1024), lambda i, s: (0, j, 0, 0), pipeline_mode=pl.Buffered(1))
    one = pl.BlockSpec((1, 128, 1024), lambda i, s: (j, 0, 0), pipeline_mode=pl.Buffered(1))
    return pl.pallas_call(
        partial_kernel,
        out_shape=(shape, shape),
        grid_spec=pltpu.PrefetchScalarGridSpec(
            num_scalar_prefetch=1,
            grid=(640 // rows,),
            in_specs=[block, block, two, two, two, one, one] + [ANY] * len(deps),
            out_specs=(out, out),
            scratch_shapes=[pltpu.VMEM((1024, 1024), jnp.bfloat16)],
        ),
        compiler_params=params(56),
        cost_estimate=cost(4 * 640 * 1024 * 1024, 8 * MIB),
        name="partial",
    )(scalars, own, sib, *ws, *deps)


def slot_table():
    rows = []
    for ylo, z, yhi in np.ndindex(2, 4, 2):
        qs = [(ylo ^ dy) * 4 + (z + dz) % 4 for dy, dz in ORDER]
        rows.append([((q % 2) ^ yhi) * 4 + q // 2 for q in qs] + [qs.index(q) for q in range(8)])
    return np.array(rows, np.int32)


SLOTS = slot_table()


def body(
    tokens,
    norm_gain,
    up_master,
    up_gradient,
    up_first,
    up_second,
    down_master,
    down_gradient,
    down_first,
    down_second,
):
    ylo, z, core, x, yhi = (lax.axis_index(a) for a in AXES)

    tokens_b = send(tokens, yhi=1)
    feats_a = lax.all_gather(tokens, "x", axis=0)

    down_args = (down_master, down_gradient, down_first, down_second)
    down_half, down_a = down_step(0, down_args)
    ylo_a = send(down_a, ylo=1)
    up_updated, columns = up_step(up_master, up_gradient, up_first, up_second, down_a)
    ylo_a = after(ylo_a, columns)
    down_updated, down_b = down_step(1, down_args, (down_half,), (ylo_a,))

    st_a = jnp.stack([down_a, ylo_a])
    low_a, high_a = both_ways(st_a, st_a)
    u0 = lax.all_to_all(columns, ("core", "x", "yhi"), 0, 0, tiled=True).reshape(512, 1024)
    u0 = after(u0, down_b, low_a, high_a)
    opp_a = both_ways(low_a[0], high_a[1])
    ws_a = (st_a, low_a, high_a, *opp_a)

    u1 = send(u0, ylo=1)
    low0, high0 = both_ways(u0, u0)
    feats_b = lax.all_gather(after(tokens_b, low0, high0, u1, *opp_a), "x", axis=0)
    down_b = after(down_b, u1)
    ylo_b = send(down_b, ylo=1)
    low1, high1 = both_ways(u1, u1)
    opp0 = both_ways(after(low0[:256], u1, *opp_a), high0[256:])
    opp1 = both_ways(low1[:256], high1[256:])
    st_b = after(jnp.stack([down_b, ylo_b]), low1)
    low_b, high_b = both_ways(st_b, st_b)

    gains = norm_gain.reshape(4, 2, 512)
    gains = jnp.concatenate([lax.dynamic_index_in_dim(gains, k, 1, keepdims=False) for k in (yhi, 1 - yhi)])
    feats_a, feats_b = feats_a.reshape(4, 640, 512), feats_b.reshape(4, 640, 512)
    normed = norm_of(feats_a, feats_b, gains, (low1, high1, *opp0, ylo_b))
    normed_sib = send(normed, core=1)

    where = lax.dynamic_index_in_dim(jnp.asarray(SLOTS), (ylo * 4 + z) * 2 + yhi, 0, keepdims=False)
    ws_up = (u0, u1, low0, low1, high0, high1)
    firsts = [hidden_first(where, n, ws_up) for n in (normed, normed_sib)]
    hidden_sib = hidden_last(where, firsts[1], normed_sib, opp0 + opp1, firsts[:1])
    hidden_own = hidden_last(where, firsts[0], normed, opp0 + opp1, (hidden_sib, low_b, high_b))
    ws_b = (st_b, low_b, high_b, *both_ways(low_b[0], high_b[1]))

    pieces, parts, sums, reduced = [], [], [], []
    places = jnp.arange(4, dtype=jnp.int32)
    add = lambda a, b: (a.astype(jnp.float32) + b.astype(jnp.float32)).astype(jnp.bfloat16)
    for j in range(CHUNKS):
        direct = j % 2 == 1
        part, part_sib = partial_of(
            (places - x) % 4 if direct else places,
            hidden_own,
            hidden_sib,
            ws_a if j < 2 else ws_b,
            j % 2,
            parts[-1:] + (sums + reduced if j == 2 else []),
        )
        parts.append(part_sib)
        part_sib = send(part_sib, core=1)
        if direct:
            terms = [add(part[d], part_sib[d]) for d in range(4)]
            sums.append(terms[1])
            terms = terms[:1] + [send(terms[d], x=d) for d in (1, 2, 3)]
            rows = sum(v.astype(jnp.float32) for v in terms).astype(jnp.bfloat16)
            reduced.append(rows)
        else:
            both = add(part, part_sib)
            sums.append(both)
            rows = lax.psum_scatter(both, "x", scatter_dimension=0, tiled=True)[0]
        keep = lax.dynamic_slice_in_dim(rows, yhi * 128, 128, 1)
        give = lax.dynamic_slice_in_dim(rows, (1 - yhi) * 128, 128, 1)
        pieces.append(add(keep, send(give, yhi=1)))
    decoded = jnp.concatenate(pieces, axis=1).reshape(2, 320, 512)
    return (up_updated, down_updated, decoded)


def solution(mesh):
    fine = Mesh(mesh.devices.reshape(SIZES), AXES)
    grp, tp = AXES[:3], AXES[3:]
    flat = P(AXES, None)
    in_specs = (P(None, grp, tp), P()) + (flat,) * 8
    out_specs = (flat, flat, P(None, grp, tp))
    return jax.shard_map(body, mesh=fine, in_specs=in_specs, out_specs=out_specs, check_vma=False)
```

```python
import functools

import jax
import jax.numpy as jnp
import numpy as np
from jax import lax
from jax.experimental import pallas as pl
from jax.experimental.pallas import tpu as pltpu
from jax.sharding import Mesh, PartitionSpec as P

learn_rate = 0.05
beta_one = 0.9
beta_two = 0.95
adam_eps = 1e-08
decay_rate = 0.1
step_index = 100
norm_eps = 1e-06

AXES = ("ylo", "z", "core", "x", "yhi")
SIZES = (2, 4, 2, 4, 2)
D, FF = 4096, 16384
CHUNKS = 4
ORDER = ((0, 0), (1, 0), (0, 3), (1, 3), (0, 1), (1, 1), (0, 2), (1, 2))
MIB = 1 << 20


def shifted(**steps):
    pairs = []
    for i, c in enumerate(np.ndindex(*SIZES)):
        d = dict(zip(AXES, c))
        for a, s in steps.items():
            d[a] = (d[a] + s) % SIZES[AXES.index(a)]
        pairs.append((i, int(np.ravel_multi_index(tuple(d[a] for a in AXES), SIZES))))
    return pairs


def send(v, **steps):
    return lax.ppermute(v, AXES, shifted(**steps))


ANY = pl.BlockSpec(memory_space=pl.ANY)


def after(v, *deps):
    return pl.pallas_call(
        lambda *refs: None,
        out_shape=jax.ShapeDtypeStruct(v.shape, v.dtype),
        in_specs=[ANY] * (1 + len(deps)),
        out_specs=ANY,
        input_output_aliases={0: 0},
        cost_estimate=pl.CostEstimate(flops=0, bytes_accessed=0, transcendentals=0),
        name="after",
    )(v, *deps)


def adamw(master, gradient, first_moment, second_moment):
    grad_float = gradient.astype(jnp.float32)
    first_new = beta_one * first_moment + (1.0 - beta_one) * grad_float
    second_new = beta_two * second_moment + (1.0 - beta_two) * grad_float * grad_float
    corr_one = 1.0 - beta_one**step_index
    corr_two = 1.0 - beta_two**step_index
    update = first_new * (1.0 / corr_one) / (jnp.sqrt(second_new * (1.0 / corr_two)) + adam_eps)
    return master - learn_rate * (update + decay_rate * master)


def params(limit=32):
    return pltpu.CompilerParams(vmem_limit_bytes=limit * MIB)


def cost(flops, nbytes):
    return pl.CostEstimate(flops=int(flops) // 1000, bytes_accessed=int(nbytes) // 1000, transcendentals=0)


def up_kernel(w_ref, g_ref, m_ref, v_ref, dep_ref, o_ref, out_ref):
    new = adamw(w_ref[...], g_ref[...], m_ref[...], v_ref[...])
    o_ref[...] = new
    cast = new.astype(jnp.bfloat16)
    for n in range(16):
        out_ref[n] = cast[:, n * 128 : (n + 1) * 128]


def up_step(w, g, m, v, dep):
    spec = pl.BlockSpec((32, 2048), lambda i: (0, i))
    return pl.pallas_call(
        up_kernel,
        out_shape=(
            jax.ShapeDtypeStruct((32, FF), jnp.float32),
            jax.ShapeDtypeStruct((16, 32, 1024), jnp.bfloat16),
        ),
        grid=(8,),
        in_specs=[spec] * 4 + [ANY],
        out_specs=(spec, pl.BlockSpec((16, 32, 128), lambda i: (0, 0, i))),
        compiler_params=params(56),
        cost_estimate=cost(30 * 32 * FF, 20 * 32 * FF),
        name="adam_up",
    )(w, g, m, v, dep)


def down_kernel(w_ref, g_ref, m_ref, v_ref, *refs):
    o_ref, d_ref = refs[-2:]
    new = adamw(w_ref[...], g_ref[...], m_ref[...], v_ref[...])
    o_ref[...] = new
    cast = new.astype(jnp.bfloat16)
    d_ref[0] = cast[:, :128]
    d_ref[1] = cast[:, 128:]


def down_step(half, args, done=(), deps=()):
    spec = pl.BlockSpec((128, 256), lambda i: (0, 2 * i + half))
    return pl.pallas_call(
        down_kernel,
        out_shape=(
            jax.ShapeDtypeStruct((128, D), jnp.float32),
            jax.ShapeDtypeStruct((2, 128, 1024), jnp.bfloat16),
        ),
        grid=(8,),
        in_specs=[spec] * 4 + [ANY] * (len(done) + len(deps)),
        out_specs=(spec, pl.BlockSpec((2, 128, 128), lambda i: (0, 0, i))),
        input_output_aliases={4: 0} if done else {},
        compiler_params=params(56),
        cost_estimate=cost(15 * 128 * D, 10 * 128 * D),
        name="adam_down",
    )(*args, *done, *deps)


def both_ways(up, down):
    return send(up, z=1), send(down, z=-1)


def norm_kernel(a_ref, b_ref, g_ref, *refs):
    out = refs[-1]
    blocks = [ref[i] for ref in (a_ref, b_ref) for i in range(4)]
    total = 0.0
    for block in blocks:
        f = block.astype(jnp.float32)
        total += jnp.sum(f * f, axis=-1, keepdims=True)
    scale = lax.rsqrt(total * (1.0 / D) + norm_eps)
    for n, block in enumerate(blocks):
        out[n] = (block.astype(jnp.float32) * scale * g_ref[n : n + 1]).astype(jnp.bfloat16)


def norm_of(feats_a, feats_b, gains, deps=()):
    rows = 160
    block = pl.BlockSpec((4, rows, 512), lambda i: (0, i, 0))
    return pl.pallas_call(
        norm_kernel,
        out_shape=jax.ShapeDtypeStruct((8, 640, 512), jnp.bfloat16),
        grid=(640 // rows,),
        in_specs=[block, block, pl.BlockSpec((8, 512), lambda i: (0, 0))] + [ANY] * len(deps),
        out_specs=pl.BlockSpec((8, rows, 512), lambda i: (0, i, 0)),
        compiler_params=params(),
        cost_estimate=cost(8 * 640 * D, 10 * MIB),
        name="norm",
    )(feats_a, feats_b, gains, *deps)


def silu(u):
    return u / (1.0 + jnp.exp(-u))


def first_kernel(s_ref, *refs):
    lhs, ws, acc = refs[:6], refs[6:12], refs[12]
    for k, (a, w) in enumerate(zip(lhs, ws)):
        term = jnp.dot(a[0], w[...], preferred_element_type=jnp.float32)
        if k == 0:
            acc[...] = term
        else:
            acc[...] += term


def last_kernel(s_ref, acc_ref, *refs):
    lhs, ws, out = refs[:2], refs[2:6], refs[-1]
    for n in range(4):
        at = slice(n * 256, (n + 1) * 256)
        u = acc_ref[:, at]
        for k, w in enumerate(ws):
            a = lhs[k // 2][0, :, (k % 2) * 256 : (k % 2 + 1) * 256]
            u += jnp.dot(a, w[:, at], preferred_element_type=jnp.float32)
        h = silu(u * D ** (-0.5)).astype(jnp.bfloat16)
        for q in (2 * n, 2 * n + 1):
            to = pl.multiple_of(s_ref[8 + q] * 128, 128)
            out[:, pl.ds(to, 128)] = h[:, (q - 2 * n) * 128 : (q - 2 * n + 1) * 128]


def hidden_specs(places, ws):
    rows = 320
    lhs = [pl.BlockSpec((1, rows, 512), functools.partial(lambda k, i, s: (s[k], i, 0), k)) for k in places]
    return lhs, [pl.BlockSpec(w.shape, lambda i, s: (0, 0), pipeline_mode=pl.Buffered(1)) for w in ws]


def hidden_first(scalars, normed, ws):
    lhs, rhs = hidden_specs(range(6), ws)
    return pl.pallas_call(
        first_kernel,
        out_shape=jax.ShapeDtypeStruct((640, 1024), jnp.float32),
        grid_spec=pltpu.PrefetchScalarGridSpec(
            num_scalar_prefetch=1,
            grid=(2,),
            in_specs=lhs + rhs,
            out_specs=pl.BlockSpec((320, 1024), lambda i, s: (i, 0)),
        ),
        compiler_params=params(),
        cost_estimate=cost(2 * 640 * 1024 * 3072, 14 * MIB),
        name="hidden_first",
    )(scalars, *([normed] * 6), *ws)


def hidden_last(scalars, acc, normed, ws, deps):
    lhs, rhs = hidden_specs((6, 7), ws)
    block = pl.BlockSpec((320, 1024), lambda i, s: (i, 0))
    return pl.pallas_call(
        last_kernel,
        out_shape=jax.ShapeDtypeStruct((640, 1024), jnp.bfloat16),
        grid_spec=pltpu.PrefetchScalarGridSpec(
            num_scalar_prefetch=1,
            grid=(2,),
            in_specs=[block] + lhs + rhs + [ANY] * len(deps),
            out_specs=block,
        ),
        compiler_params=params(),
        cost_estimate=cost(2 * 640 * 1024 * 1024, 8 * MIB),
        name="hidden_last",
    )(scalars, acc, normed, normed, *ws, *deps)


def partial_kernel(s_ref, own_ref, sib_ref, *refs):
    ws, (own_out, sib_out, w_ref) = refs[:5], refs[-3:]

    @pl.when(pl.program_id(0) == 0)
    def _():
        at = 0
        for w in ws:
            for part in [w[0, 0], w[1, 0]] if len(w.shape) == 4 else [w[0]]:
                w_ref[at : at + 128] = part
                at += 128

    for src, dst in ((sib_ref, sib_out), (own_ref, own_out)):
        term = jnp.dot(src[...], w_ref[...], preferred_element_type=jnp.float32)
        term = (term * FF ** (-0.5)).astype(jnp.bfloat16)
        for xi in range(4):
            dst[s_ref[xi]] = term[:, xi * 256 : (xi + 1) * 256]


def partial_of(scalars, own, sib, ws, j, deps):
    rows = 320
    block = pl.BlockSpec((rows, 1024), lambda i, s: (i, 0))
    out = pl.BlockSpec((4, rows, 256), lambda i, s: (0, i, 0))
    shape = jax.ShapeDtypeStruct((4, 640, 256), jnp.bfloat16)
    two = pl.BlockSpec((2, 1, 128, 1024), lambda i, s: (0, j, 0, 0), pipeline_mode=pl.Buffered(1))
    one = pl.BlockSpec((1, 128, 1024), lambda i, s: (j, 0, 0), pipeline_mode=pl.Buffered(1))
    return pl.pallas_call(
        partial_kernel,
        out_shape=(shape, shape),
        grid_spec=pltpu.PrefetchScalarGridSpec(
            num_scalar_prefetch=1,
            grid=(640 // rows,),
            in_specs=[block, block, two, two, two, one, one] + [ANY] * len(deps),
            out_specs=(out, out),
            scratch_shapes=[pltpu.VMEM((1024, 1024), jnp.bfloat16)],
        ),
        compiler_params=params(56),
        cost_estimate=cost(4 * 640 * 1024 * 1024, 8 * MIB),
        name="partial",
    )(scalars, own, sib, *ws, *deps)


def slot_table():
    rows = []
    for ylo, z, yhi in np.ndindex(2, 4, 2):
        qs = [(ylo ^ dy) * 4 + (z + dz) % 4 for dy, dz in ORDER]
        rows.append([((q % 2) ^ yhi) * 4 + q // 2 for q in qs] + [qs.index(q) for q in range(8)])
    return np.array(rows, np.int32)


SLOTS = slot_table()


def body(
    tokens,
    norm_gain,
    up_master,
    up_gradient,
    up_first,
    up_second,
    down_master,
    down_gradient,
    down_first,
    down_second,
):
    ylo, z, core, x, yhi = (lax.axis_index(a) for a in AXES)

    tokens_b = send(tokens, yhi=1)
    feats_a = lax.all_gather(tokens, "x", axis=0)

    down_args = (down_master, down_gradient, down_first, down_second)
    down_half, down_a = down_step(0, down_args)
    ylo_a = send(down_a, ylo=1)
    up_updated, columns = up_step(up_master, up_gradient, up_first, up_second, down_a)
    ylo_a = after(ylo_a, columns)
    down_updated, down_b = down_step(1, down_args, (down_half,), (ylo_a,))

    st_a = jnp.stack([down_a, ylo_a])
    low_a, high_a = both_ways(st_a, st_a)
    u0 = lax.all_to_all(columns, ("core", "x", "yhi"), 0, 0, tiled=True).reshape(512, 1024)
    u0 = after(u0, down_b, low_a, high_a)
    opp_a = both_ways(low_a[0], high_a[1])
    ws_a = (st_a, low_a, high_a, *opp_a)

    u1 = send(u0, ylo=1)
    low0, high0 = both_ways(u0, u0)
    feats_b = lax.all_gather(after(tokens_b, low0, high0, u1, *opp_a), "x", axis=0)
    down_b = after(down_b, u1)
    ylo_b = send(down_b, ylo=1)
    low1, high1 = both_ways(u1, u1)
    opp0 = both_ways(after(low0[:256], u1, *opp_a), high0[256:])
    opp1 = both_ways(low1[:256], high1[256:])
    st_b = after(jnp.stack([down_b, ylo_b]), low1)
    low_b, high_b = both_ways(st_b, st_b)

    gains = norm_gain.reshape(4, 2, 512)
    gains = jnp.concatenate([lax.dynamic_index_in_dim(gains, k, 1, keepdims=False) for k in (yhi, 1 - yhi)])
    feats_a, feats_b = feats_a.reshape(4, 640, 512), feats_b.reshape(4, 640, 512)
    normed = norm_of(feats_a, feats_b, gains, (low1, high1, *opp0, ylo_b))
    normed_sib = send(normed, core=1)

    where = lax.dynamic_index_in_dim(jnp.asarray(SLOTS), (ylo * 4 + z) * 2 + yhi, 0, keepdims=False)
    ws_up = (u0, u1, low0, low1, high0, high1)
    firsts = [hidden_first(where, n, ws_up) for n in (normed, normed_sib)]
    hidden_sib = hidden_last(where, firsts[1], normed_sib, opp0 + opp1, firsts[:1])
    hidden_own = hidden_last(where, firsts[0], normed, opp0 + opp1, (hidden_sib, low_b, high_b))
    ws_b = (st_b, low_b, high_b, *both_ways(low_b[0], high_b[1]))

    pieces, parts, sums, near = [], [], [], []
    places = jnp.arange(4, dtype=jnp.int32)
    add = lambda a, b: (a.astype(jnp.float32) + b.astype(jnp.float32)).astype(jnp.bfloat16)
    for j in range(CHUNKS):
        direct = j in (0, 3)
        part, part_sib = partial_of(
            (places - x) % 4 if direct else places,
            hidden_own,
            hidden_sib,
            ws_a if j < 2 else ws_b,
            j % 2,
            parts[-1:] + ([], [], sums[1:] + near, [])[j],
        )
        parts.append(part_sib)
        part_sib = send(part_sib, core=1)
        if direct:
            terms = [add(part[d], part_sib[d]) for d in range(4)]
            sums.append(terms[1])
            terms = terms[:1] + [send(terms[d], x=d) for d in (1, 2, 3)]
            near = terms[3:]
            rows = sum(v.astype(jnp.float32) for v in terms).astype(jnp.bfloat16)
        else:
            both = add(part, part_sib)
            sums.append(both)
            rows = lax.psum_scatter(both, "x", scatter_dimension=0, tiled=True)[0]
        pieces.append(rows)
    halves = []
    for pair in (pieces[:2], pieces[2:]):
        keep = [lax.dynamic_slice_in_dim(v, yhi * 128, 128, 1) for v in pair]
        give = jnp.stack([lax.dynamic_slice_in_dim(v, (1 - yhi) * 128, 128, 1) for v in pair])
        got = send(give, yhi=1)
        halves += [add(k, got[n]) for n, k in enumerate(keep)]
    decoded = jnp.concatenate(halves, axis=1).reshape(2, 320, 512)
    return (up_updated, down_updated, decoded)


def solution(mesh):
    fine = Mesh(mesh.devices.reshape(SIZES), AXES)
    grp, tp = AXES[:3], AXES[3:]
    flat = P(AXES, None)
    in_specs = (P(None, grp, tp), P()) + (flat,) * 8
    out_specs = (flat, flat, P(None, grp, tp))
    return jax.shard_map(body, mesh=fine, in_specs=in_specs, out_specs=out_specs, check_vma=False)
```

```python
import functools

import jax
import jax.numpy as jnp
import numpy as np
from jax import lax
from jax.experimental import pallas as pl
from jax.experimental.pallas import tpu as pltpu
from jax.sharding import Mesh, PartitionSpec as P

learn_rate = 0.05
beta_one = 0.9
beta_two = 0.95
adam_eps = 1e-08
decay_rate = 0.1
step_index = 100
norm_eps = 1e-06

AXES = ("ylo", "z", "core", "x", "yhi")
SIZES = (2, 4, 2, 4, 2)
D, FF = 4096, 16384
CHUNKS = 4
ORDER = ((0, 0), (1, 0), (0, 3), (1, 3), (0, 1), (1, 1), (0, 2), (1, 2))
MIB = 1 << 20


def shifted(**steps):
    pairs = []
    for i, c in enumerate(np.ndindex(*SIZES)):
        d = dict(zip(AXES, c))
        for a, s in steps.items():
            d[a] = (d[a] + s) % SIZES[AXES.index(a)]
        pairs.append((i, int(np.ravel_multi_index(tuple(d[a] for a in AXES), SIZES))))
    return pairs


def send(v, **steps):
    return lax.ppermute(v, AXES, shifted(**steps))


ANY = pl.BlockSpec(memory_space=pl.ANY)


def after(v, *deps):
    return pl.pallas_call(
        lambda *refs: None,
        out_shape=jax.ShapeDtypeStruct(v.shape, v.dtype),
        in_specs=[ANY] * (1 + len(deps)),
        out_specs=ANY,
        input_output_aliases={0: 0},
        cost_estimate=pl.CostEstimate(flops=0, bytes_accessed=0, transcendentals=0),
        name="after",
    )(v, *deps)


def adamw(master, gradient, first_moment, second_moment):
    grad_float = gradient.astype(jnp.float32)
    first_new = beta_one * first_moment + (1.0 - beta_one) * grad_float
    second_new = beta_two * second_moment + (1.0 - beta_two) * grad_float * grad_float
    corr_one = 1.0 - beta_one**step_index
    corr_two = 1.0 - beta_two**step_index
    update = first_new * (1.0 / corr_one) / (jnp.sqrt(second_new * (1.0 / corr_two)) + adam_eps)
    return master - learn_rate * (update + decay_rate * master)


def params(limit=32):
    return pltpu.CompilerParams(vmem_limit_bytes=limit * MIB)


def cost(flops, nbytes):
    return pl.CostEstimate(flops=int(flops) // 1000, bytes_accessed=int(nbytes) // 1000, transcendentals=0)


def up_kernel(w_ref, g_ref, m_ref, v_ref, dep_ref, o_ref, out_ref):
    new = adamw(w_ref[...], g_ref[...], m_ref[...], v_ref[...])
    o_ref[...] = new
    cast = new.astype(jnp.bfloat16)
    for n in range(16):
        out_ref[n] = cast[:, n * 128 : (n + 1) * 128]


def up_step(w, g, m, v, dep):
    spec = pl.BlockSpec((32, 2048), lambda i: (0, i))
    return pl.pallas_call(
        up_kernel,
        out_shape=(
            jax.ShapeDtypeStruct((32, FF), jnp.float32),
            jax.ShapeDtypeStruct((16, 32, 1024), jnp.bfloat16),
        ),
        grid=(8,),
        in_specs=[spec] * 4 + [ANY],
        out_specs=(spec, pl.BlockSpec((16, 32, 128), lambda i: (0, 0, i))),
        compiler_params=params(56),
        cost_estimate=cost(30 * 32 * FF, 20 * 32 * FF),
        name="adam_up",
    )(w, g, m, v, dep)


def down_kernel(w_ref, g_ref, m_ref, v_ref, *refs):
    o_ref, d_ref = refs[-2:]
    new = adamw(w_ref[...], g_ref[...], m_ref[...], v_ref[...])
    o_ref[...] = new
    cast = new.astype(jnp.bfloat16)
    d_ref[0] = cast[:, :128]
    d_ref[1] = cast[:, 128:]


def down_step(half, args, done=(), deps=()):
    spec = pl.BlockSpec((128, 256), lambda i: (0, 2 * i + half))
    return pl.pallas_call(
        down_kernel,
        out_shape=(
            jax.ShapeDtypeStruct((128, D), jnp.float32),
            jax.ShapeDtypeStruct((2, 128, 1024), jnp.bfloat16),
        ),
        grid=(8,),
        in_specs=[spec] * 4 + [ANY] * (len(done) + len(deps)),
        out_specs=(spec, pl.BlockSpec((2, 128, 128), lambda i: (0, 0, i))),
        input_output_aliases={4: 0} if done else {},
        compiler_params=params(56),
        cost_estimate=cost(15 * 128 * D, 10 * 128 * D),
        name="adam_down",
    )(*args, *done, *deps)


def both_ways(up, down):
    return send(up, z=1), send(down, z=-1)


def norm_kernel(a_ref, b_ref, g_ref, *refs):
    out = refs[-1]
    blocks = [ref[i] for ref in (a_ref, b_ref) for i in range(4)]
    total = 0.0
    for block in blocks:
        f = block.astype(jnp.float32)
        total += jnp.sum(f * f, axis=-1, keepdims=True)
    scale = lax.rsqrt(total * (1.0 / D) + norm_eps)
    for n, block in enumerate(blocks):
        out[n] = (block.astype(jnp.float32) * scale * g_ref[n : n + 1]).astype(jnp.bfloat16)


def norm_of(feats_a, feats_b, gains, deps=()):
    rows = 160
    block = pl.BlockSpec((4, rows, 512), lambda i: (0, i, 0))
    return pl.pallas_call(
        norm_kernel,
        out_shape=jax.ShapeDtypeStruct((8, 640, 512), jnp.bfloat16),
        grid=(640 // rows,),
        in_specs=[block, block, pl.BlockSpec((8, 512), lambda i: (0, 0))] + [ANY] * len(deps),
        out_specs=pl.BlockSpec((8, rows, 512), lambda i: (0, i, 0)),
        compiler_params=params(),
        cost_estimate=cost(8 * 640 * D, 10 * MIB),
        name="norm",
    )(feats_a, feats_b, gains, *deps)


def silu(u):
    return u / (1.0 + jnp.exp(-u))


def first_kernel(s_ref, *refs):
    lhs, ws, acc = refs[:6], refs[6:12], refs[12]
    for k, (a, w) in enumerate(zip(lhs, ws)):
        term = jnp.dot(a[0], w[...], preferred_element_type=jnp.float32)
        if k == 0:
            acc[...] = term
        else:
            acc[...] += term


def last_kernel(s_ref, acc_ref, *refs):
    lhs, ws, out = refs[:2], refs[2:6], refs[-1]
    for n in range(4):
        at = slice(n * 256, (n + 1) * 256)
        u = acc_ref[:, at]
        for k, w in enumerate(ws):
            a = lhs[k // 2][0, :, (k % 2) * 256 : (k % 2 + 1) * 256]
            u += jnp.dot(a, w[:, at], preferred_element_type=jnp.float32)
        h = silu(u * D ** (-0.5)).astype(jnp.bfloat16)
        for q in (2 * n, 2 * n + 1):
            to = pl.multiple_of(s_ref[8 + q] * 128, 128)
            out[:, pl.ds(to, 128)] = h[:, (q - 2 * n) * 128 : (q - 2 * n + 1) * 128]


def hidden_specs(places, ws):
    rows = 320
    lhs = [pl.BlockSpec((1, rows, 512), functools.partial(lambda k, i, s: (s[k], i, 0), k)) for k in places]
    return lhs, [pl.BlockSpec(w.shape, lambda i, s: (0, 0), pipeline_mode=pl.Buffered(1)) for w in ws]


def hidden_first(scalars, normed, ws):
    lhs, rhs = hidden_specs(range(6), ws)
    return pl.pallas_call(
        first_kernel,
        out_shape=jax.ShapeDtypeStruct((640, 1024), jnp.float32),
        grid_spec=pltpu.PrefetchScalarGridSpec(
            num_scalar_prefetch=1,
            grid=(2,),
            in_specs=lhs + rhs,
            out_specs=pl.BlockSpec((320, 1024), lambda i, s: (i, 0)),
        ),
        compiler_params=params(),
        cost_estimate=cost(2 * 640 * 1024 * 3072, 14 * MIB),
        name="hidden_first",
    )(scalars, *([normed] * 6), *ws)


def hidden_last(scalars, acc, normed, ws, deps):
    lhs, rhs = hidden_specs((6, 7), ws)
    block = pl.BlockSpec((320, 1024), lambda i, s: (i, 0))
    return pl.pallas_call(
        last_kernel,
        out_shape=jax.ShapeDtypeStruct((640, 1024), jnp.bfloat16),
        grid_spec=pltpu.PrefetchScalarGridSpec(
            num_scalar_prefetch=1,
            grid=(2,),
            in_specs=[block] + lhs + rhs + [ANY] * len(deps),
            out_specs=block,
        ),
        compiler_params=params(),
        cost_estimate=cost(2 * 640 * 1024 * 1024, 8 * MIB),
        name="hidden_last",
    )(scalars, acc, normed, normed, *ws, *deps)


def partial_kernel(s_ref, own_ref, sib_ref, *refs):
    ws, (own_out, sib_out, w_ref) = refs[:5], refs[-3:]

    @pl.when(pl.program_id(0) == 0)
    def _():
        at = 0
        for w in ws:
            for part in [w[0, 0], w[1, 0]] if len(w.shape) == 4 else [w[0]]:
                w_ref[at : at + 128] = part
                at += 128

    for src, dst in ((sib_ref, sib_out), (own_ref, own_out)):
        term = jnp.dot(src[...], w_ref[...], preferred_element_type=jnp.float32)
        term = (term * FF ** (-0.5)).astype(jnp.bfloat16)
        for xi in range(4):
            dst[s_ref[xi]] = term[:, xi * 256 : (xi + 1) * 256]


def partial_of(scalars, own, sib, ws, j, deps):
    rows = 320
    block = pl.BlockSpec((rows, 1024), lambda i, s: (i, 0))
    out = pl.BlockSpec((4, rows, 256), lambda i, s: (0, i, 0))
    shape = jax.ShapeDtypeStruct((4, 640, 256), jnp.bfloat16)
    two = pl.BlockSpec((2, 1, 128, 1024), lambda i, s: (0, j, 0, 0), pipeline_mode=pl.Buffered(1))
    one = pl.BlockSpec((1, 128, 1024), lambda i, s: (j, 0, 0), pipeline_mode=pl.Buffered(1))
    return pl.pallas_call(
        partial_kernel,
        out_shape=(shape, shape),
        grid_spec=pltpu.PrefetchScalarGridSpec(
            num_scalar_prefetch=1,
            grid=(640 // rows,),
            in_specs=[block, block, two, two, two, one, one] + [ANY] * len(deps),
            out_specs=(out, out),
            scratch_shapes=[pltpu.VMEM((1024, 1024), jnp.bfloat16)],
        ),
        compiler_params=params(56),
        cost_estimate=cost(4 * 640 * 1024 * 1024, 8 * MIB),
        name="partial",
    )(scalars, own, sib, *ws, *deps)


def slot_table():
    rows = []
    for ylo, z, yhi in np.ndindex(2, 4, 2):
        qs = [(ylo ^ dy) * 4 + (z + dz) % 4 for dy, dz in ORDER]
        rows.append([((q % 2) ^ yhi) * 4 + q // 2 for q in qs] + [qs.index(q) for q in range(8)])
    return np.array(rows, np.int32)


SLOTS = slot_table()


def body(
    tokens,
    norm_gain,
    up_master,
    up_gradient,
    up_first,
    up_second,
    down_master,
    down_gradient,
    down_first,
    down_second,
):
    ylo, z, core, x, yhi = (lax.axis_index(a) for a in AXES)

    tokens_b = send(tokens, yhi=1)
    feats_a = lax.all_gather(tokens, "x", axis=0)

    down_args = (down_master, down_gradient, down_first, down_second)
    down_half, down_a = down_step(0, down_args)
    ylo_a = send(down_a, ylo=1)
    up_updated, columns = up_step(up_master, up_gradient, up_first, up_second, down_a)
    ylo_a = after(ylo_a, columns)
    down_updated, down_b = down_step(1, down_args, (down_half,), (ylo_a,))

    st_a = jnp.stack([down_a, ylo_a])
    low_a, high_a = both_ways(st_a, st_a)
    u0 = lax.all_to_all(columns, ("core", "x", "yhi"), 0, 0, tiled=True).reshape(512, 1024)
    u0 = after(u0, down_b, low_a, high_a)
    opp_a = both_ways(low_a[0], high_a[1])
    ws_a = (st_a, low_a, high_a, *opp_a)

    u1 = send(u0, ylo=1)
    low0, high0 = both_ways(u0, u0)
    feats_b = lax.all_gather(after(tokens_b, low0, high0, u1, *opp_a), "x", axis=0)
    down_b = after(down_b, u1)
    ylo_b = send(down_b, ylo=1)
    low1, high1 = both_ways(u1, u1)
    opp0 = both_ways(after(low0[:256], u1, *opp_a), high0[256:])
    opp1 = tuple(send(o, ylo=1) for o in opp0)
    st_b = after(jnp.stack([down_b, ylo_b]), low1)
    low_b, high_b = both_ways(st_b, st_b)

    gains = norm_gain.reshape(4, 2, 512)
    gains = jnp.concatenate([lax.dynamic_index_in_dim(gains, k, 1, keepdims=False) for k in (yhi, 1 - yhi)])
    feats_a, feats_b = feats_a.reshape(4, 640, 512), feats_b.reshape(4, 640, 512)
    normed = norm_of(feats_a, feats_b, gains, (low1, high1, *opp0, ylo_b))
    normed_sib = send(normed, core=1)

    where = lax.dynamic_index_in_dim(jnp.asarray(SLOTS), (ylo * 4 + z) * 2 + yhi, 0, keepdims=False)
    ws_up = (u0, u1, low0, low1, high0, high1)
    firsts = [hidden_first(where, n, ws_up) for n in (normed, normed_sib)]
    hidden_sib = hidden_last(where, firsts[1], normed_sib, opp0 + opp1, firsts[:1])
    hidden_own = hidden_last(where, firsts[0], normed, opp0 + opp1, (hidden_sib, low_b, high_b))
    ws_b = (st_b, low_b, high_b, *both_ways(low_b[0], high_b[1]))

    pieces, parts, sums, reduced, gots = [], [], [], [], []
    places = jnp.arange(4, dtype=jnp.int32)
    add = lambda a, b: (a.astype(jnp.float32) + b.astype(jnp.float32)).astype(jnp.bfloat16)
    for j in range(CHUNKS):
        direct = j % 2 == 1
        part, part_sib = partial_of(
            (places - x) % 4 if direct else places,
            hidden_own,
            hidden_sib,
            ws_a if j < 2 else ws_b,
            j % 2,
            parts[-1:] + ([], [], sums + reduced, gots[:2])[j],
        )
        parts.append(part_sib)
        part_sib = send(part_sib, core=1)
        if direct:
            terms = [add(part[d], part_sib[d]) for d in range(4)]
            sums.append(terms[1])
            terms = terms[:1] + [send(terms[d], x=d) for d in (1, 2, 3)]
            rows = sum(v.astype(jnp.float32) for v in terms).astype(jnp.bfloat16)
            reduced.append(rows)
        else:
            both = add(part, part_sib)
            sums.append(both)
            rows = lax.psum_scatter(both, "x", scatter_dimension=0, tiled=True)[0]
        keep = lax.dynamic_slice_in_dim(rows, yhi * 128, 128, 1)
        give = lax.dynamic_slice_in_dim(rows, (1 - yhi) * 128, 128, 1)
        gots.append(send(give, yhi=1))
        pieces.append(add(keep, gots[-1]))
    decoded = jnp.concatenate(pieces, axis=1).reshape(2, 320, 512)
    return (up_updated, down_updated, decoded)


def solution(mesh):
    fine = Mesh(mesh.devices.reshape(SIZES), AXES)
    grp, tp = AXES[:3], AXES[3:]
    flat = P(AXES, None)
    in_specs = (P(None, grp, tp), P()) + (flat,) * 8
    out_specs = (flat, flat, P(None, grp, tp))
    return jax.shard_map(body, mesh=fine, in_specs=in_specs, out_specs=out_specs, check_vma=False)
```

```python
import functools

import jax
import jax.numpy as jnp
import numpy as np
from jax import lax
from jax.experimental import pallas as pl
from jax.experimental.pallas import tpu as pltpu
from jax.sharding import Mesh, PartitionSpec as P

learn_rate = 0.05
beta_one = 0.9
beta_two = 0.95
adam_eps = 1e-08
decay_rate = 0.1
step_index = 100
norm_eps = 1e-06

AXES = ("ylo", "z", "core", "x", "yhi")
SIZES = (2, 4, 2, 4, 2)
D, FF = 4096, 16384
CHUNKS = 4
ORDER = ((0, 0), (1, 0), (0, 3), (1, 3), (0, 1), (1, 1), (0, 2), (1, 2))
MIB = 1 << 20


def shifted(**steps):
    pairs = []
    for i, c in enumerate(np.ndindex(*SIZES)):
        d = dict(zip(AXES, c))
        for a, s in steps.items():
            d[a] = (d[a] + s) % SIZES[AXES.index(a)]
        pairs.append((i, int(np.ravel_multi_index(tuple(d[a] for a in AXES), SIZES))))
    return pairs


def send(v, **steps):
    return lax.ppermute(v, AXES, shifted(**steps))


ANY = pl.BlockSpec(memory_space=pl.ANY)


def after(v, *deps):
    return pl.pallas_call(
        lambda *refs: None,
        out_shape=jax.ShapeDtypeStruct(v.shape, v.dtype),
        in_specs=[ANY] * (1 + len(deps)),
        out_specs=ANY,
        input_output_aliases={0: 0},
        cost_estimate=pl.CostEstimate(flops=0, bytes_accessed=0, transcendentals=0),
        name="after",
    )(v, *deps)


def adamw(master, gradient, first_moment, second_moment):
    grad_float = gradient.astype(jnp.float32)
    first_new = beta_one * first_moment + (1.0 - beta_one) * grad_float
    second_new = beta_two * second_moment + (1.0 - beta_two) * grad_float * grad_float
    corr_one = 1.0 - beta_one**step_index
    corr_two = 1.0 - beta_two**step_index
    update = first_new * (1.0 / corr_one) / (jnp.sqrt(second_new * (1.0 / corr_two)) + adam_eps)
    return master - learn_rate * (update + decay_rate * master)


def params(limit=32):
    return pltpu.CompilerParams(vmem_limit_bytes=limit * MIB)


def cost(flops, nbytes):
    return pl.CostEstimate(flops=int(flops) // 1000, bytes_accessed=int(nbytes) // 1000, transcendentals=0)


def up_kernel(w_ref, g_ref, m_ref, v_ref, dep_ref, o_ref, out_ref):
    new = adamw(w_ref[...], g_ref[...], m_ref[...], v_ref[...])
    o_ref[...] = new
    cast = new.astype(jnp.bfloat16)
    for n in range(16):
        out_ref[n] = cast[:, n * 128 : (n + 1) * 128]


def up_step(w, g, m, v, dep):
    spec = pl.BlockSpec((32, 2048), lambda i: (0, i))
    return pl.pallas_call(
        up_kernel,
        out_shape=(
            jax.ShapeDtypeStruct((32, FF), jnp.float32),
            jax.ShapeDtypeStruct((16, 32, 1024), jnp.bfloat16),
        ),
        grid=(8,),
        in_specs=[spec] * 4 + [ANY],
        out_specs=(spec, pl.BlockSpec((16, 32, 128), lambda i: (0, 0, i))),
        compiler_params=params(56),
        cost_estimate=cost(30 * 32 * FF, 20 * 32 * FF),
        name="adam_up",
    )(w, g, m, v, dep)


def down_kernel(w_ref, g_ref, m_ref, v_ref, *refs):
    o_ref, d_ref = refs[-2:]
    new = adamw(w_ref[...], g_ref[...], m_ref[...], v_ref[...])
    o_ref[...] = new
    cast = new.astype(jnp.bfloat16)
    d_ref[0] = cast[:, :128]
    d_ref[1] = cast[:, 128:]


def down_step(half, args, done=(), deps=()):
    spec = pl.BlockSpec((128, 256), lambda i: (0, 2 * i + half))
    return pl.pallas_call(
        down_kernel,
        out_shape=(
            jax.ShapeDtypeStruct((128, D), jnp.float32),
            jax.ShapeDtypeStruct((2, 128, 1024), jnp.bfloat16),
        ),
        grid=(8,),
        in_specs=[spec] * 4 + [ANY] * (len(done) + len(deps)),
        out_specs=(spec, pl.BlockSpec((2, 128, 128), lambda i: (0, 0, i))),
        input_output_aliases={4: 0} if done else {},
        compiler_params=params(56),
        cost_estimate=cost(15 * 128 * D, 10 * 128 * D),
        name="adam_down",
    )(*args, *done, *deps)


def both_ways(up, down):
    return send(up, z=1), send(down, z=-1)


def norm_kernel(a_ref, b_ref, g_ref, *refs):
    out = refs[-1]
    blocks = [ref[i] for ref in (a_ref, b_ref) for i in range(4)]
    total = 0.0
    for block in blocks:
        f = block.astype(jnp.float32)
        total += jnp.sum(f * f, axis=-1, keepdims=True)
    scale = lax.rsqrt(total * (1.0 / D) + norm_eps)
    for n, block in enumerate(blocks):
        out[n] = (block.astype(jnp.float32) * scale * g_ref[n : n + 1]).astype(jnp.bfloat16)


def norm_of(feats_a, feats_b, gains, deps=()):
    rows = 160
    block = pl.BlockSpec((4, rows, 512), lambda i: (0, i, 0))
    return pl.pallas_call(
        norm_kernel,
        out_shape=jax.ShapeDtypeStruct((8, 640, 512), jnp.bfloat16),
        grid=(640 // rows,),
        in_specs=[block, block, pl.BlockSpec((8, 512), lambda i: (0, 0))] + [ANY] * len(deps),
        out_specs=pl.BlockSpec((8, rows, 512), lambda i: (0, i, 0)),
        compiler_params=params(56),
        cost_estimate=cost(8 * 640 * D, 10 * MIB),
        name="norm",
    )(feats_a, feats_b, gains, *deps)


def silu(u):
    return u / (1.0 + jnp.exp(-u))


def first_kernel(s_ref, *refs):
    lhs, ws, acc = refs[:6], refs[6:12], refs[12]
    for k, (a, w) in enumerate(zip(lhs, ws)):
        term = jnp.dot(a[0], w[...], preferred_element_type=jnp.float32)
        if k == 0:
            acc[...] = term
        else:
            acc[...] += term


def last_kernel(s_ref, acc_ref, *refs):
    lhs, ws, out = refs[:2], refs[2:6], refs[-1]
    for n in range(4):
        at = slice(n * 256, (n + 1) * 256)
        u = acc_ref[:, at]
        for k, w in enumerate(ws):
            a = lhs[k // 2][0, :, (k % 2) * 256 : (k % 2 + 1) * 256]
            u += jnp.dot(a, w[:, at], preferred_element_type=jnp.float32)
        h = silu(u * D ** (-0.5)).astype(jnp.bfloat16)
        for q in (2 * n, 2 * n + 1):
            to = pl.multiple_of(s_ref[8 + q] * 128, 128)
            out[:, pl.ds(to, 128)] = h[:, (q - 2 * n) * 128 : (q - 2 * n + 1) * 128]


def hidden_specs(places, ws):
    rows = 320
    lhs = [pl.BlockSpec((1, rows, 512), functools.partial(lambda k, i, s: (s[k], i, 0), k)) for k in places]
    return lhs, [pl.BlockSpec(w.shape, lambda i, s: (0, 0), pipeline_mode=pl.Buffered(1)) for w in ws]


def hidden_first(scalars, normed, ws):
    lhs, rhs = hidden_specs(range(6), ws)
    return pl.pallas_call(
        first_kernel,
        out_shape=jax.ShapeDtypeStruct((640, 1024), jnp.float32),
        grid_spec=pltpu.PrefetchScalarGridSpec(
            num_scalar_prefetch=1,
            grid=(2,),
            in_specs=lhs + rhs,
            out_specs=pl.BlockSpec((320, 1024), lambda i, s: (i, 0)),
        ),
        compiler_params=params(),
        cost_estimate=cost(2 * 640 * 1024 * 3072, 14 * MIB),
        name="hidden_first",
    )(scalars, *([normed] * 6), *ws)


def hidden_last(scalars, acc, normed, ws, deps):
    lhs, rhs = hidden_specs((6, 7), ws)
    block = pl.BlockSpec((320, 1024), lambda i, s: (i, 0))
    return pl.pallas_call(
        last_kernel,
        out_shape=jax.ShapeDtypeStruct((640, 1024), jnp.bfloat16),
        grid_spec=pltpu.PrefetchScalarGridSpec(
            num_scalar_prefetch=1,
            grid=(2,),
            in_specs=[block] + lhs + rhs + [ANY] * len(deps),
            out_specs=block,
        ),
        compiler_params=params(),
        cost_estimate=cost(2 * 640 * 1024 * 1024, 8 * MIB),
        name="hidden_last",
    )(scalars, acc, normed, normed, *ws, *deps)


def partial_kernel(s_ref, own_ref, sib_ref, *refs):
    ws, (own_out, sib_out, w_ref) = refs[:5], refs[-3:]

    @pl.when(pl.program_id(0) == 0)
    def _():
        at = 0
        for w in ws:
            for part in [w[0, 0], w[1, 0]] if len(w.shape) == 4 else [w[0]]:
                w_ref[at : at + 128] = part
                at += 128

    for src, dst in ((sib_ref, sib_out), (own_ref, own_out)):
        term = jnp.dot(src[...], w_ref[...], preferred_element_type=jnp.float32)
        term = (term * FF ** (-0.5)).astype(jnp.bfloat16)
        for xi in range(4):
            dst[s_ref[xi]] = term[:, xi * 256 : (xi + 1) * 256]


def partial_of(scalars, own, sib, ws, j, deps):
    rows = 320
    block = pl.BlockSpec((rows, 1024), lambda i, s: (i, 0))
    out = pl.BlockSpec((4, rows, 256), lambda i, s: (0, i, 0))
    shape = jax.ShapeDtypeStruct((4, 640, 256), jnp.bfloat16)
    two = pl.BlockSpec((2, 1, 128, 1024), lambda i, s: (0, j, 0, 0), pipeline_mode=pl.Buffered(1))
    one = pl.BlockSpec((1, 128, 1024), lambda i, s: (j, 0, 0), pipeline_mode=pl.Buffered(1))
    return pl.pallas_call(
        partial_kernel,
        out_shape=(shape, shape),
        grid_spec=pltpu.PrefetchScalarGridSpec(
            num_scalar_prefetch=1,
            grid=(640 // rows,),
            in_specs=[block, block, two, two, two, one, one] + [ANY] * len(deps),
            out_specs=(out, out),
            scratch_shapes=[pltpu.VMEM((1024, 1024), jnp.bfloat16)],
        ),
        compiler_params=params(56),
        cost_estimate=cost(4 * 640 * 1024 * 1024, 8 * MIB),
        name="partial",
    )(scalars, own, sib, *ws, *deps)


def slot_table():
    rows = []
    for ylo, z, yhi in np.ndindex(2, 4, 2):
        qs = [(ylo ^ dy) * 4 + (z + dz) % 4 for dy, dz in ORDER]
        rows.append([((q % 2) ^ yhi) * 4 + q // 2 for q in qs] + [qs.index(q) for q in range(8)])
    return np.array(rows, np.int32)


SLOTS = slot_table()


def body(
    tokens,
    norm_gain,
    up_master,
    up_gradient,
    up_first,
    up_second,
    down_master,
    down_gradient,
    down_first,
    down_second,
):
    ylo, z, core, x, yhi = (lax.axis_index(a) for a in AXES)

    tokens_b = send(tokens, yhi=1)
    feats_a = lax.all_gather(tokens, "x", axis=0)

    down_args = (down_master, down_gradient, down_first, down_second)
    down_half, down_a = down_step(0, down_args)
    ylo_a = send(down_a, ylo=1)
    up_updated, columns = up_step(up_master, up_gradient, up_first, up_second, down_a)
    ylo_a = after(ylo_a, columns)
    down_updated, down_b = down_step(1, down_args, (down_half,), (ylo_a,))

    st_a = jnp.stack([down_a, ylo_a])
    low_a, high_a = both_ways(st_a, st_a)
    u0 = lax.all_to_all(columns, ("core", "x", "yhi"), 0, 0, tiled=True).reshape(512, 1024)
    u0 = after(u0, down_b, low_a, high_a)
    opp_a = both_ways(low_a[0], high_a[1])
    ws_a = (st_a, low_a, high_a, *opp_a)

    u1 = send(u0, ylo=1)
    low0, high0 = both_ways(u0, u0)
    feats_b = lax.all_gather(after(tokens_b, low0, high0, u1, *opp_a), "x", axis=0)
    down_b = after(down_b, u1)
    ylo_b = send(down_b, ylo=1)
    low1, high1 = both_ways(u1, u1)
    opp0 = both_ways(after(low0[:256], u1, *opp_a), high0[256:])
    opp1 = tuple(send(o, ylo=1) for o in opp0)
    st_b = after(jnp.stack([down_b, ylo_b]), low1)
    low_b, high_b = both_ways(st_b, st_b)

    gains = norm_gain.reshape(4, 2, 512)
    gains = jnp.concatenate([lax.dynamic_index_in_dim(gains, k, 1, keepdims=False) for k in (yhi, 1 - yhi)])
    feats_a, feats_b = feats_a.reshape(4, 640, 512), feats_b.reshape(4, 640, 512)
    normed = norm_of(feats_a, feats_b, gains, (low1, high1, *opp0, ylo_b))
    normed_sib = send(normed, core=1)

    where = lax.dynamic_index_in_dim(jnp.asarray(SLOTS), (ylo * 4 + z) * 2 + yhi, 0, keepdims=False)
    ws_up = (u0, u1, low0, low1, high0, high1)
    firsts = [hidden_first(where, n, ws_up) for n in (normed, normed_sib)]
    hidden_sib = hidden_last(where, firsts[1], normed_sib, opp0 + opp1, firsts[:1])
    hidden_own = hidden_last(where, firsts[0], normed, opp0 + opp1, (hidden_sib, low_b, high_b))
    ws_b = (st_b, low_b, high_b, *both_ways(low_b[0], high_b[1]))

    pieces, parts, sums, reduced, gots = [], [], [], [], []
    places = jnp.arange(4, dtype=jnp.int32)
    add = lambda a, b: (a.astype(jnp.float32) + b.astype(jnp.float32)).astype(jnp.bfloat16)
    for j in range(CHUNKS):
        direct = j % 2 == 1
        part, part_sib = partial_of(
            (places - x) % 4 if direct else places,
            hidden_own,
            hidden_sib,
            ws_a if j < 2 else ws_b,
            j % 2,
            parts[-1:] + ([], [], sums + reduced, [])[j],
        )
        parts.append(part_sib)
        part_sib = send(part_sib, core=1)
        if direct:
            terms = [add(part[d], part_sib[d]) for d in range(4)]
            sums.append(terms[1])
            terms = terms[:1] + [send(terms[d], x=d) for d in (1, 2, 3)]
            rows = sum(v.astype(jnp.float32) for v in terms).astype(jnp.bfloat16)
            reduced.append(rows)
        else:
            both = add(part, part_sib)
            sums.append(both)
            rows = lax.psum_scatter(both, "x", scatter_dimension=0, tiled=True)[0]
        keep = lax.dynamic_slice_in_dim(rows, yhi * 128, 128, 1)
        give = lax.dynamic_slice_in_dim(rows, (1 - yhi) * 128, 128, 1)
        gots.append(send(after(give, *gots[:2]) if j == 3 else give, yhi=1))
        pieces.append(add(keep, gots[-1]))
    decoded = jnp.concatenate(pieces, axis=1).reshape(2, 320, 512)
    return (up_updated, down_updated, decoded)


def solution(mesh):
    fine = Mesh(mesh.devices.reshape(SIZES), AXES)
    grp, tp = AXES[:3], AXES[3:]
    flat = P(AXES, None)
    in_specs = (P(None, grp, tp), P()) + (flat,) * 8
    out_specs = (flat, flat, P(None, grp, tp))
    return jax.shard_map(body, mesh=fine, in_specs=in_specs, out_specs=out_specs, check_vma=False)
```

```python
import functools

import jax
import jax.numpy as jnp
import numpy as np
from jax import lax
from jax.experimental import pallas as pl
from jax.experimental.pallas import tpu as pltpu
from jax.sharding import Mesh, PartitionSpec as P

learn_rate = 0.05
beta_one = 0.9
beta_two = 0.95
adam_eps = 1e-08
decay_rate = 0.1
step_index = 100
norm_eps = 1e-06

AXES = ("ylo", "z", "core", "x", "yhi")
SIZES = (2, 4, 2, 4, 2)
D, FF = 4096, 16384
CHUNKS = 4
ORDER = ((0, 0), (1, 0), (0, 3), (1, 3), (0, 1), (1, 1), (0, 2), (1, 2))
MIB = 1 << 20


def shifted(**steps):
    pairs = []
    for i, c in enumerate(np.ndindex(*SIZES)):
        d = dict(zip(AXES, c))
        for a, s in steps.items():
            d[a] = (d[a] + s) % SIZES[AXES.index(a)]
        pairs.append((i, int(np.ravel_multi_index(tuple(d[a] for a in AXES), SIZES))))
    return pairs


def send(v, **steps):
    return lax.ppermute(v, AXES, shifted(**steps))


ANY = pl.BlockSpec(memory_space=pl.ANY)


def after(v, *deps):
    return pl.pallas_call(
        lambda *refs: None,
        out_shape=jax.ShapeDtypeStruct(v.shape, v.dtype),
        in_specs=[ANY] * (1 + len(deps)),
        out_specs=ANY,
        input_output_aliases={0: 0},
        cost_estimate=pl.CostEstimate(flops=0, bytes_accessed=0, transcendentals=0),
        name="after",
    )(v, *deps)


def adamw(master, gradient, first_moment, second_moment):
    grad_float = gradient.astype(jnp.float32)
    first_new = beta_one * first_moment + (1.0 - beta_one) * grad_float
    second_new = beta_two * second_moment + (1.0 - beta_two) * grad_float * grad_float
    corr_one = 1.0 - beta_one**step_index
    corr_two = 1.0 - beta_two**step_index
    update = first_new * (1.0 / corr_one) / (jnp.sqrt(second_new * (1.0 / corr_two)) + adam_eps)
    return master - learn_rate * (update + decay_rate * master)


def params(limit=32):
    return pltpu.CompilerParams(vmem_limit_bytes=limit * MIB)


def cost(flops, nbytes):
    return pl.CostEstimate(flops=int(flops) // 1000, bytes_accessed=int(nbytes) // 1000, transcendentals=0)


def up_kernel(w_ref, g_ref, m_ref, v_ref, dep_ref, o_ref, out_ref):
    new = adamw(w_ref[...], g_ref[...], m_ref[...], v_ref[...])
    o_ref[...] = new
    cast = new.astype(jnp.bfloat16)
    for n in range(16):
        out_ref[n] = cast[:, n * 128 : (n + 1) * 128]


def up_step(w, g, m, v, dep):
    spec = pl.BlockSpec((32, 2048), lambda i: (0, i))
    return pl.pallas_call(
        up_kernel,
        out_shape=(
            jax.ShapeDtypeStruct((32, FF), jnp.float32),
            jax.ShapeDtypeStruct((16, 32, 1024), jnp.bfloat16),
        ),
        grid=(8,),
        in_specs=[spec] * 4 + [ANY],
        out_specs=(spec, pl.BlockSpec((16, 32, 128), lambda i: (0, 0, i))),
        compiler_params=params(56),
        cost_estimate=cost(30 * 32 * FF, 20 * 32 * FF),
        name="adam_up",
    )(w, g, m, v, dep)


def down_kernel(w_ref, g_ref, m_ref, v_ref, *refs):
    o_ref, d_ref = refs[-2:]
    new = adamw(w_ref[...], g_ref[...], m_ref[...], v_ref[...])
    o_ref[...] = new
    cast = new.astype(jnp.bfloat16)
    d_ref[0] = cast[:, :128]
    d_ref[1] = cast[:, 128:]


def down_step(half, args, done=(), deps=()):
    spec = pl.BlockSpec((128, 256), lambda i: (0, 2 * i + half))
    return pl.pallas_call(
        down_kernel,
        out_shape=(
            jax.ShapeDtypeStruct((128, D), jnp.float32),
            jax.ShapeDtypeStruct((2, 128, 1024), jnp.bfloat16),
        ),
        grid=(8,),
        in_specs=[spec] * 4 + [ANY] * (len(done) + len(deps)),
        out_specs=(spec, pl.BlockSpec((2, 128, 128), lambda i: (0, 0, i))),
        input_output_aliases={4: 0} if done else {},
        compiler_params=params(56),
        cost_estimate=cost(15 * 128 * D, 10 * 128 * D),
        name="adam_down",
    )(*args, *done, *deps)


def both_ways(up, down):
    return send(up, z=1), send(down, z=-1)


def norm_kernel(a_ref, b_ref, g_ref, *refs):
    out = refs[-1]
    blocks = [ref[i] for ref in (a_ref, b_ref) for i in range(4)]
    total = 0.0
    for block in blocks:
        f = block.astype(jnp.float32)
        total += jnp.sum(f * f, axis=-1, keepdims=True)
    scale = lax.rsqrt(total * (1.0 / D) + norm_eps)
    for n, block in enumerate(blocks):
        out[n] = (block.astype(jnp.float32) * scale * g_ref[n : n + 1]).astype(jnp.bfloat16)


def norm_of(feats_a, feats_b, gains, deps=()):
    rows = 160
    block = pl.BlockSpec((4, rows, 512), lambda i: (0, i, 0))
    return pl.pallas_call(
        norm_kernel,
        out_shape=jax.ShapeDtypeStruct((8, 640, 512), jnp.bfloat16),
        grid=(640 // rows,),
        in_specs=[block, block, pl.BlockSpec((8, 512), lambda i: (0, 0))] + [ANY] * len(deps),
        out_specs=pl.BlockSpec((8, rows, 512), lambda i: (0, i, 0)),
        compiler_params=params(56),
        cost_estimate=cost(8 * 640 * D, 10 * MIB),
        name="norm",
    )(feats_a, feats_b, gains, *deps)


def silu(u):
    return u / (1.0 + jnp.exp(-u))


def first_kernel(s_ref, *refs):
    lhs, ws, acc = refs[:6], refs[6:12], refs[12]
    for k, (a, w) in enumerate(zip(lhs, ws)):
        term = jnp.dot(a[0], w[...], preferred_element_type=jnp.float32)
        if k == 0:
            acc[...] = term
        else:
            acc[...] += term


def last_kernel(s_ref, acc_ref, *refs):
    lhs, ws, out = refs[:2], refs[2:6], refs[-1]
    for n in range(4):
        at = slice(n * 256, (n + 1) * 256)
        u = acc_ref[:, at]
        for k, w in enumerate(ws):
            a = lhs[k // 2][0, :, (k % 2) * 256 : (k % 2 + 1) * 256]
            u += jnp.dot(a, w[:, at], preferred_element_type=jnp.float32)
        h = silu(u * D ** (-0.5)).astype(jnp.bfloat16)
        for q in (2 * n, 2 * n + 1):
            to = pl.multiple_of(s_ref[8 + q] * 128, 128)
            out[:, pl.ds(to, 128)] = h[:, (q - 2 * n) * 128 : (q - 2 * n + 1) * 128]


def hidden_specs(places, ws):
    rows = 320
    lhs = [pl.BlockSpec((1, rows, 512), functools.partial(lambda k, i, s: (s[k], i, 0), k)) for k in places]
    return lhs, [pl.BlockSpec(w.shape, lambda i, s: (0, 0), pipeline_mode=pl.Buffered(1)) for w in ws]


def hidden_first(scalars, normed, ws):
    lhs, rhs = hidden_specs(range(6), ws)
    return pl.pallas_call(
        first_kernel,
        out_shape=jax.ShapeDtypeStruct((640, 1024), jnp.float32),
        grid_spec=pltpu.PrefetchScalarGridSpec(
            num_scalar_prefetch=1,
            grid=(2,),
            in_specs=lhs + rhs,
            out_specs=pl.BlockSpec((320, 1024), lambda i, s: (i, 0)),
        ),
        compiler_params=params(),
        cost_estimate=cost(2 * 640 * 1024 * 3072, 14 * MIB),
        name="hidden_first",
    )(scalars, *([normed] * 6), *ws)


def hidden_last(scalars, acc, normed, ws, deps):
    lhs, rhs = hidden_specs((6, 7), ws)
    block = pl.BlockSpec((320, 1024), lambda i, s: (i, 0))
    return pl.pallas_call(
        last_kernel,
        out_shape=jax.ShapeDtypeStruct((640, 1024), jnp.bfloat16),
        grid_spec=pltpu.PrefetchScalarGridSpec(
            num_scalar_prefetch=1,
            grid=(2,),
            in_specs=[block] + lhs + rhs + [ANY] * len(deps),
            out_specs=block,
        ),
        compiler_params=params(),
        cost_estimate=cost(2 * 640 * 1024 * 1024, 8 * MIB),
        name="hidden_last",
    )(scalars, acc, normed, normed, *ws, *deps)


def partial_kernel(s_ref, own_ref, sib_ref, *refs):
    ws, (own_out, sib_out, w_ref) = refs[:5], refs[-3:]

    @pl.when(pl.program_id(0) == 0)
    def _():
        at = 0
        for w in ws:
            for part in [w[0, 0], w[1, 0]] if len(w.shape) == 4 else [w[0]]:
                w_ref[at : at + 128] = part
                at += 128

    for src, dst in ((sib_ref, sib_out), (own_ref, own_out)):
        term = jnp.dot(src[...], w_ref[...], preferred_element_type=jnp.float32)
        term = (term * FF ** (-0.5)).astype(jnp.bfloat16)
        for xi in range(4):
            dst[s_ref[xi]] = term[:, xi * 256 : (xi + 1) * 256]


def partial_of(scalars, own, sib, ws, j, deps):
    rows = 320
    block = pl.BlockSpec((rows, 1024), lambda i, s: (i, 0))
    out = pl.BlockSpec((4, rows, 256), lambda i, s: (0, i, 0))
    shape = jax.ShapeDtypeStruct((4, 640, 256), jnp.bfloat16)
    two = pl.BlockSpec((2, 1, 128, 1024), lambda i, s: (0, j, 0, 0), pipeline_mode=pl.Buffered(1))
    one = pl.BlockSpec((1, 128, 1024), lambda i, s: (j, 0, 0), pipeline_mode=pl.Buffered(1))
    return pl.pallas_call(
        partial_kernel,
        out_shape=(shape, shape),
        grid_spec=pltpu.PrefetchScalarGridSpec(
            num_scalar_prefetch=1,
            grid=(640 // rows,),
            in_specs=[block, block, two, two, two, one, one] + [ANY] * len(deps),
            out_specs=(out, out),
            scratch_shapes=[pltpu.VMEM((1024, 1024), jnp.bfloat16)],
        ),
        compiler_params=params(56),
        cost_estimate=cost(4 * 640 * 1024 * 1024, 8 * MIB),
        name="partial",
    )(scalars, own, sib, *ws, *deps)


def slot_table():
    rows = []
    for ylo, z, yhi in np.ndindex(2, 4, 2):
        qs = [(ylo ^ dy) * 4 + (z + dz) % 4 for dy, dz in ORDER]
        rows.append([((q % 2) ^ yhi) * 4 + q // 2 for q in qs] + [qs.index(q) for q in range(8)])
    return np.array(rows, np.int32)


SLOTS = slot_table()


def body(
    tokens,
    norm_gain,
    up_master,
    up_gradient,
    up_first,
    up_second,
    down_master,
    down_gradient,
    down_first,
    down_second,
):
    ylo, z, core, x, yhi = (lax.axis_index(a) for a in AXES)

    tokens_b = send(tokens, yhi=1)
    feats_a = lax.all_gather(tokens, "x", axis=0)

    down_args = (down_master, down_gradient, down_first, down_second)
    down_half, down_a = down_step(0, down_args)
    ylo_a = send(down_a, ylo=1)
    up_updated, columns = up_step(up_master, up_gradient, up_first, up_second, down_a)
    ylo_a = after(ylo_a, columns, tokens_b)
    down_updated, down_b = down_step(1, down_args, (down_half,), (ylo_a,))

    st_a = jnp.stack([down_a, ylo_a])
    low_a, high_a = both_ways(st_a, st_a)
    u0 = lax.all_to_all(columns, ("core", "x", "yhi"), 0, 0, tiled=True).reshape(512, 1024)
    u0 = after(u0, down_b, low_a, high_a)
    opp_a = both_ways(low_a[0], high_a[1])
    ws_a = (st_a, low_a, high_a, *opp_a)

    u1 = send(u0, ylo=1)
    low0, high0 = both_ways(u0, u0)
    feats_b = lax.all_gather(after(tokens_b, u0), "x", axis=0)
    down_b = after(down_b, u1)
    ylo_b = send(down_b, ylo=1)
    low1, high1 = both_ways(u1, u1)
    opp0 = both_ways(after(low0[:256], u1, *opp_a), high0[256:])
    opp1 = tuple(send(o, ylo=1) for o in opp0)
    st_b = after(jnp.stack([down_b, ylo_b]), low1)
    low_b, high_b = both_ways(st_b, st_b)

    gains = norm_gain.reshape(4, 2, 512)
    gains = jnp.concatenate([lax.dynamic_index_in_dim(gains, k, 1, keepdims=False) for k in (yhi, 1 - yhi)])
    feats_a, feats_b = feats_a.reshape(4, 640, 512), feats_b.reshape(4, 640, 512)
    normed = norm_of(feats_a, feats_b, gains, (low0, high0, u1, *opp_a))
    normed_sib = send(normed, core=1)

    where = lax.dynamic_index_in_dim(jnp.asarray(SLOTS), (ylo * 4 + z) * 2 + yhi, 0, keepdims=False)
    ws_up = (u0, u1, low0, low1, high0, high1)
    firsts = [hidden_first(where, n, ws_up) for n in (normed, normed_sib)]
    hidden_sib = hidden_last(where, firsts[1], normed_sib, opp0 + opp1, firsts[:1])
    hidden_own = hidden_last(where, firsts[0], normed, opp0 + opp1, (hidden_sib, low_b, high_b))
    ws_b = (st_b, low_b, high_b, *both_ways(low_b[0], high_b[1]))

    pieces, parts, sums, reduced, gots = [], [], [], [], []
    places = jnp.arange(4, dtype=jnp.int32)
    add = lambda a, b: (a.astype(jnp.float32) + b.astype(jnp.float32)).astype(jnp.bfloat16)
    for j in range(CHUNKS):
        direct = j % 2 == 1
        part, part_sib = partial_of(
            (places - x) % 4 if direct else places,
            hidden_own,
            hidden_sib,
            ws_a if j < 2 else ws_b,
            j % 2,
            parts[-1:] + ([], [], sums + reduced, [])[j],
        )
        parts.append(part_sib)
        part_sib = send(part_sib, core=1)
        if direct:
            terms = [add(part[d], part_sib[d]) for d in range(4)]
            sums.append(terms[1])
            terms = terms[:1] + [send(terms[d], x=d) for d in (1, 2, 3)]
            rows = sum(v.astype(jnp.float32) for v in terms).astype(jnp.bfloat16)
            reduced.append(rows)
        else:
            both = add(part, part_sib)
            sums.append(both)
            rows = lax.psum_scatter(both, "x", scatter_dimension=0, tiled=True)[0]
        keep = lax.dynamic_slice_in_dim(rows, yhi * 128, 128, 1)
        give = lax.dynamic_slice_in_dim(rows, (1 - yhi) * 128, 128, 1)
        gots.append(send(after(give, *gots[:2]) if j == 3 else give, yhi=1))
        pieces.append(add(keep, gots[-1]))
    decoded = jnp.concatenate(pieces, axis=1).reshape(2, 320, 512)
    return (up_updated, down_updated, decoded)


def solution(mesh):
    fine = Mesh(mesh.devices.reshape(SIZES), AXES)
    grp, tp = AXES[:3], AXES[3:]
    flat = P(AXES, None)
    in_specs = (P(None, grp, tp), P()) + (flat,) * 8
    out_specs = (flat, flat, P(None, grp, tp))
    return jax.shard_map(body, mesh=fine, in_specs=in_specs, out_specs=out_specs, check_vma=False)
```

```python
import functools

import jax
import jax.numpy as jnp
import numpy as np
from jax import lax
from jax.experimental import pallas as pl
from jax.experimental.pallas import tpu as pltpu
from jax.sharding import Mesh, PartitionSpec as P

learn_rate = 0.05
beta_one = 0.9
beta_two = 0.95
adam_eps = 1e-08
decay_rate = 0.1
step_index = 100
norm_eps = 1e-06

AXES = ("ylo", "z", "core", "x", "yhi")
SIZES = (2, 4, 2, 4, 2)
D, FF = 4096, 16384
CHUNKS = 4
ORDER = ((0, 0), (1, 0), (0, 3), (1, 3), (0, 1), (1, 1), (0, 2), (1, 2))
MIB = 1 << 20


def shifted(**steps):
    pairs = []
    for i, c in enumerate(np.ndindex(*SIZES)):
        d = dict(zip(AXES, c))
        for a, s in steps.items():
            d[a] = (d[a] + s) % SIZES[AXES.index(a)]
        pairs.append((i, int(np.ravel_multi_index(tuple(d[a] for a in AXES), SIZES))))
    return pairs


def send(v, **steps):
    return lax.ppermute(v, AXES, shifted(**steps))


ANY = pl.BlockSpec(memory_space=pl.ANY)


def after(v, *deps):
    return pl.pallas_call(
        lambda *refs: None,
        out_shape=jax.ShapeDtypeStruct(v.shape, v.dtype),
        in_specs=[ANY] * (1 + len(deps)),
        out_specs=ANY,
        input_output_aliases={0: 0},
        cost_estimate=pl.CostEstimate(flops=0, bytes_accessed=0, transcendentals=0),
        name="after",
    )(v, *deps)


def adamw(master, gradient, first_moment, second_moment):
    grad_float = gradient.astype(jnp.float32)
    first_new = beta_one * first_moment + (1.0 - beta_one) * grad_float
    second_new = beta_two * second_moment + (1.0 - beta_two) * grad_float * grad_float
    corr_one = 1.0 - beta_one**step_index
    corr_two = 1.0 - beta_two**step_index
    update = first_new * (1.0 / corr_one) / (jnp.sqrt(second_new * (1.0 / corr_two)) + adam_eps)
    return master - learn_rate * (update + decay_rate * master)


def params(limit=32):
    return pltpu.CompilerParams(vmem_limit_bytes=limit * MIB)


def cost(flops, nbytes):
    return pl.CostEstimate(flops=int(flops) // 1000, bytes_accessed=int(nbytes) // 1000, transcendentals=0)


def up_kernel(w_ref, g_ref, m_ref, v_ref, dep_ref, o_ref, out_ref):
    new = adamw(w_ref[...], g_ref[...], m_ref[...], v_ref[...])
    o_ref[...] = new
    cast = new.astype(jnp.bfloat16)
    for n in range(16):
        out_ref[n] = cast[:, n * 128 : (n + 1) * 128]


def up_step(w, g, m, v, dep):
    spec = pl.BlockSpec((32, 2048), lambda i: (0, i))
    return pl.pallas_call(
        up_kernel,
        out_shape=(
            jax.ShapeDtypeStruct((32, FF), jnp.float32),
            jax.ShapeDtypeStruct((16, 32, 1024), jnp.bfloat16),
        ),
        grid=(8,),
        in_specs=[spec] * 4 + [ANY],
        out_specs=(spec, pl.BlockSpec((16, 32, 128), lambda i: (0, 0, i))),
        compiler_params=params(56),
        cost_estimate=cost(30 * 32 * FF, 20 * 32 * FF),
        name="adam_up",
    )(w, g, m, v, dep)


def down_kernel(w_ref, g_ref, m_ref, v_ref, *refs):
    o_ref, d_ref = refs[-2:]
    new = adamw(w_ref[...], g_ref[...], m_ref[...], v_ref[...])
    o_ref[...] = new
    cast = new.astype(jnp.bfloat16)
    d_ref[0] = cast[:, :128]
    d_ref[1] = cast[:, 128:]


def down_step(half, args, done=(), deps=()):
    spec = pl.BlockSpec((128, 256), lambda i: (0, 2 * i + half))
    return pl.pallas_call(
        down_kernel,
        out_shape=(
            jax.ShapeDtypeStruct((128, D), jnp.float32),
            jax.ShapeDtypeStruct((2, 128, 1024), jnp.bfloat16),
        ),
        grid=(8,),
        in_specs=[spec] * 4 + [ANY] * (len(done) + len(deps)),
        out_specs=(spec, pl.BlockSpec((2, 128, 128), lambda i: (0, 0, i))),
        input_output_aliases={4: 0} if done else {},
        compiler_params=params(56),
        cost_estimate=cost(15 * 128 * D, 10 * 128 * D),
        name="adam_down",
    )(*args, *done, *deps)


def both_ways(up, down):
    return send(up, z=1), send(down, z=-1)


def norm_kernel(a_ref, b_ref, g_ref, *refs):
    out = refs[-1]
    blocks = [ref[i] for ref in (a_ref, b_ref) for i in range(4)]
    total = 0.0
    for block in blocks:
        f = block.astype(jnp.float32)
        total += jnp.sum(f * f, axis=-1, keepdims=True)
    scale = lax.rsqrt(total * (1.0 / D) + norm_eps)
    for n, block in enumerate(blocks):
        out[n] = (block.astype(jnp.float32) * scale * g_ref[n : n + 1]).astype(jnp.bfloat16)


def norm_of(feats_a, feats_b, gains, deps=()):
    rows = 160
    block = pl.BlockSpec((4, rows, 512), lambda i: (0, i, 0))
    return pl.pallas_call(
        norm_kernel,
        out_shape=jax.ShapeDtypeStruct((8, 640, 512), jnp.bfloat16),
        grid=(640 // rows,),
        in_specs=[block, block, pl.BlockSpec((8, 512), lambda i: (0, 0))] + [ANY] * len(deps),
        out_specs=pl.BlockSpec((8, rows, 512), lambda i: (0, i, 0)),
        compiler_params=params(56),
        cost_estimate=cost(8 * 640 * D, 10 * MIB),
        name="norm",
    )(feats_a, feats_b, gains, *deps)


def silu(u):
    return u / (1.0 + jnp.exp(-u))


def first_kernel(s_ref, *refs):
    lhs, ws, acc = refs[:6], refs[6:12], refs[12]
    for k, (a, w) in enumerate(zip(lhs, ws)):
        term = jnp.dot(a[0], w[...], preferred_element_type=jnp.float32)
        if k == 0:
            acc[...] = term
        else:
            acc[...] += term


def last_kernel(s_ref, acc_ref, *refs):
    lhs, ws, out = refs[:2], refs[2:6], refs[-1]
    for n in range(4):
        at = slice(n * 256, (n + 1) * 256)
        u = acc_ref[:, at]
        for k, w in enumerate(ws):
            a = lhs[k // 2][0, :, (k % 2) * 256 : (k % 2 + 1) * 256]
            u += jnp.dot(a, w[:, at], preferred_element_type=jnp.float32)
        h = silu(u * D ** (-0.5)).astype(jnp.bfloat16)
        for q in (2 * n, 2 * n + 1):
            to = pl.multiple_of(s_ref[8 + q] * 128, 128)
            out[:, pl.ds(to, 128)] = h[:, (q - 2 * n) * 128 : (q - 2 * n + 1) * 128]


def hidden_specs(places, ws):
    rows = 320
    lhs = [pl.BlockSpec((1, rows, 512), functools.partial(lambda k, i, s: (s[k], i, 0), k)) for k in places]
    return lhs, [pl.BlockSpec(w.shape, lambda i, s: (0, 0), pipeline_mode=pl.Buffered(1)) for w in ws]


def hidden_first(scalars, normed, ws):
    lhs, rhs = hidden_specs(range(6), ws)
    return pl.pallas_call(
        first_kernel,
        out_shape=jax.ShapeDtypeStruct((640, 1024), jnp.float32),
        grid_spec=pltpu.PrefetchScalarGridSpec(
            num_scalar_prefetch=1,
            grid=(2,),
            in_specs=lhs + rhs,
            out_specs=pl.BlockSpec((320, 1024), lambda i, s: (i, 0)),
        ),
        compiler_params=params(),
        cost_estimate=cost(2 * 640 * 1024 * 3072, 14 * MIB),
        name="hidden_first",
    )(scalars, *([normed] * 6), *ws)


def hidden_last(scalars, acc, normed, ws, deps):
    lhs, rhs = hidden_specs((6, 7), ws)
    block = pl.BlockSpec((320, 1024), lambda i, s: (i, 0))
    return pl.pallas_call(
        last_kernel,
        out_shape=jax.ShapeDtypeStruct((640, 1024), jnp.bfloat16),
        grid_spec=pltpu.PrefetchScalarGridSpec(
            num_scalar_prefetch=1,
            grid=(2,),
            in_specs=[block] + lhs + rhs + [ANY] * len(deps),
            out_specs=block,
        ),
        compiler_params=params(),
        cost_estimate=cost(2 * 640 * 1024 * 1024, 8 * MIB),
        name="hidden_last",
    )(scalars, acc, normed, normed, *ws, *deps)


def partial_kernel(s_ref, own_ref, sib_ref, *refs):
    ws, (own_out, sib_out, w_ref) = refs[:5], refs[-3:]

    @pl.when(pl.program_id(0) == 0)
    def _():
        at = 0
        for w in ws:
            for part in [w[0, 0], w[1, 0]] if len(w.shape) == 4 else [w[0]]:
                w_ref[at : at + 128] = part
                at += 128

    for src, dst in ((sib_ref, sib_out), (own_ref, own_out)):
        term = jnp.dot(src[...], w_ref[...], preferred_element_type=jnp.float32)
        term = (term * FF ** (-0.5)).astype(jnp.bfloat16)
        for xi in range(4):
            dst[s_ref[xi]] = term[:, xi * 256 : (xi + 1) * 256]


def partial_of(scalars, own, sib, ws, j, deps):
    rows = 320
    block = pl.BlockSpec((rows, 1024), lambda i, s: (i, 0))
    out = pl.BlockSpec((4, rows, 256), lambda i, s: (0, i, 0))
    shape = jax.ShapeDtypeStruct((4, 640, 256), jnp.bfloat16)
    two = pl.BlockSpec((2, 1, 128, 1024), lambda i, s: (0, j, 0, 0), pipeline_mode=pl.Buffered(1))
    one = pl.BlockSpec((1, 128, 1024), lambda i, s: (j, 0, 0), pipeline_mode=pl.Buffered(1))
    return pl.pallas_call(
        partial_kernel,
        out_shape=(shape, shape),
        grid_spec=pltpu.PrefetchScalarGridSpec(
            num_scalar_prefetch=1,
            grid=(640 // rows,),
            in_specs=[block, block, two, two, two, one, one] + [ANY] * len(deps),
            out_specs=(out, out),
            scratch_shapes=[pltpu.VMEM((1024, 1024), jnp.bfloat16)],
        ),
        compiler_params=params(56),
        cost_estimate=cost(4 * 640 * 1024 * 1024, 8 * MIB),
        name="partial",
    )(scalars, own, sib, *ws, *deps)


def slot_table():
    rows = []
    for ylo, z, yhi in np.ndindex(2, 4, 2):
        qs = [(ylo ^ dy) * 4 + (z + dz) % 4 for dy, dz in ORDER]
        rows.append([((q % 2) ^ yhi) * 4 + q // 2 for q in qs] + [qs.index(q) for q in range(8)])
    return np.array(rows, np.int32)


SLOTS = slot_table()


def body(
    tokens,
    norm_gain,
    up_master,
    up_gradient,
    up_first,
    up_second,
    down_master,
    down_gradient,
    down_first,
    down_second,
):
    ylo, z, core, x, yhi = (lax.axis_index(a) for a in AXES)

    tokens_b = send(tokens, yhi=1)
    feats_a = lax.all_gather(tokens, "x", axis=0)

    down_args = (down_master, down_gradient, down_first, down_second)
    down_half, down_a = down_step(0, down_args)
    ylo_a = send(down_a, ylo=1)
    up_updated, columns = up_step(up_master, up_gradient, up_first, up_second, down_a)
    ylo_a = after(ylo_a, columns)
    down_updated, down_b = down_step(1, down_args, (down_half,), (columns,))

    st_a = jnp.stack([down_a, ylo_a])
    low_a, high_a = both_ways(st_a, st_a)
    u0 = lax.all_to_all(columns, ("core", "x", "yhi"), 0, 0, tiled=True).reshape(512, 1024)
    u0 = after(u0, down_b)
    opp_a = both_ways(low_a[0], high_a[1])
    ws_a = (st_a, low_a, high_a, *opp_a)

    u1 = send(u0, ylo=1)
    low0, high0 = both_ways(u0, u0)
    feats_b = lax.all_gather(after(tokens_b, low0, high0, u1, *opp_a), "x", axis=0)
    down_b = after(down_b, u1)
    ylo_b = send(down_b, ylo=1)
    low1, high1 = both_ways(u1, u1)
    opp0 = both_ways(after(low0[:256], u1, *opp_a), high0[256:])
    opp1 = tuple(send(o, ylo=1) for o in opp0)
    st_b = after(jnp.stack([down_b, ylo_b]), low1)
    low_b, high_b = both_ways(st_b, st_b)

    gains = norm_gain.reshape(4, 2, 512)
    gains = jnp.concatenate([lax.dynamic_index_in_dim(gains, k, 1, keepdims=False) for k in (yhi, 1 - yhi)])
    feats_a, feats_b = feats_a.reshape(4, 640, 512), feats_b.reshape(4, 640, 512)
    normed = norm_of(feats_a, feats_b, gains, (low1, high1, *opp0, ylo_b))
    normed_sib = send(normed, core=1)

    where = lax.dynamic_index_in_dim(jnp.asarray(SLOTS), (ylo * 4 + z) * 2 + yhi, 0, keepdims=False)
    ws_up = (u0, u1, low0, low1, high0, high1)
    firsts = [hidden_first(where, n, ws_up) for n in (normed, normed_sib)]
    hidden_sib = hidden_last(where, firsts[1], normed_sib, opp0 + opp1, firsts[:1])
    hidden_own = hidden_last(where, firsts[0], normed, opp0 + opp1, (hidden_sib, low_b, high_b))
    ws_b = (st_b, low_b, high_b, *both_ways(low_b[0], high_b[1]))

    pieces, parts, sums, reduced, gots = [], [], [], [], []
    places = jnp.arange(4, dtype=jnp.int32)
    add = lambda a, b: (a.astype(jnp.float32) + b.astype(jnp.float32)).astype(jnp.bfloat16)
    for j in range(CHUNKS):
        direct = j % 2 == 1
        part, part_sib = partial_of(
            (places - x) % 4 if direct else places,
            hidden_own,
            hidden_sib,
            ws_a if j < 2 else ws_b,
            j % 2,
            parts[-1:] + ([], [], sums + reduced, [])[j],
        )
        parts.append(part_sib)
        part_sib = send(part_sib, core=1)
        if direct:
            terms = [add(part[d], part_sib[d]) for d in range(4)]
            sums.append(terms[1])
            terms = terms[:1] + [send(terms[d], x=d) for d in (1, 2, 3)]
            rows = sum(v.astype(jnp.float32) for v in terms).astype(jnp.bfloat16)
            reduced.append(rows)
        else:
            both = add(part, part_sib)
            sums.append(both)
            rows = lax.psum_scatter(both, "x", scatter_dimension=0, tiled=True)[0]
        keep = lax.dynamic_slice_in_dim(rows, yhi * 128, 128, 1)
        give = lax.dynamic_slice_in_dim(rows, (1 - yhi) * 128, 128, 1)
        gots.append(send(after(give, *gots[:2]) if j == 3 else give, yhi=1))
        pieces.append(add(keep, gots[-1]))
    decoded = jnp.concatenate(pieces, axis=1).reshape(2, 320, 512)
    return (up_updated, down_updated, decoded)


def solution(mesh):
    fine = Mesh(mesh.devices.reshape(SIZES), AXES)
    grp, tp = AXES[:3], AXES[3:]
    flat = P(AXES, None)
    in_specs = (P(None, grp, tp), P()) + (flat,) * 8
    out_specs = (flat, flat, P(None, grp, tp))
    return jax.shard_map(body, mesh=fine, in_specs=in_specs, out_specs=out_specs, check_vma=False)
```
